32 devices in a mesh: tm: 16 (over z, x, core), space: 2 (over y).
Axes of the slice: x: 2, y: 2, z: 4, core: 2. Of those that a mesh axis runs over, the one named last changes fastest.
Arguments:
- start_disp: float32 [16, 3, 4, 64, 256], P('tm', None, None, 'space'), may hold values from -0.2 to 0.2
- start_vel: float32 [16, 3, 4, 64, 256], P('tm', None, None, 'space'), may hold values from -0.2 to 0.2
- start_visc: float32 [16, 3, 4, 64, 256], P('tm', None, None, 'space'), may hold values from -0.2 to 0.2
- init_state: float32 [3, 3, 4, 64, 256], P(None, None, None, 'space'), may hold values from -0.2 to 0.2
- inv_mass: float32 [4, 64, 256], P(None, 'space'), may hold values from 0.35 to 1
- damping_rate: float32 [4, 64, 256], P(None, 'space'), may hold values from 0.002 to 0.2
- visc_rate: float32 [4, 64, 256], P(None, 'space'), may hold values from 0.02 to 2
- fiber_stiff: float32 [4, 64, 256], P(None, 'space'), may hold values from 0.05 to 0.25
- fiber_family: int32 [16, 8], P('space'), may hold values from 0 to 3
- pressure: float32 [16, 4], P('tm'), may hold values from 0.2 to 1
Outputs:
- new_disp: float32 [16, 3, 4, 64, 256], P('tm', None, None, 'space')
- new_vel: float32 [16, 3, 4, 64, 256], P('tm', None, None, 'space')
- new_visc: float32 [16, 3, 4, 64, 256], P('tm', None, None, 'space')
The draws below stay inside these ranges and needn't reach their ends.
All inputs are finite; a program needn't handle non-finite values.
Results may differ from the reference program's by a relative error of at most 0.000029.
Values sent between devices are 32-bit elements; how exact they have to be, the bound alone decides.
No kernel may reach another device: no remote copies, remote signals or barrier semaphores. Data moves between devices by JAX's collectives and lax.ppermute only.
A program may use at most 128 MiB of HBM per device.

```python
import math
import jax
import jax.numpy as jnp
from jax import lax

RAD = 4
CIR = 256
STEPS = 4
BLK_AX = 4
BLK_CIR = 32
NA = 64
SLABS = 16


def touch_ends(result, rng, low, high):
    place = [jax.random.randint(jax.random.fold_in(rng, axis), (), 0, length) for axis, length in enumerate(result.shape)]
    main_axis = result.shape.index(max(result.shape))
    beside = place[:main_axis] + [(place[main_axis] + 1) % result.shape[main_axis]] + place[main_axis + 1:]
    return result.at[tuple(place)].set(low).at[tuple(beside)].set(high)


def shard_levels(stream_key, extent, cuts, least, high):
    loudness, own = 1.0, jax.random.fold_in(stream_key, 6)
    for axis_at, parts in cuts:
        heights = jnp.exp(jax.random.uniform(jax.random.fold_in(own, axis_at), (parts,), jnp.float32, least / len(cuts), high / len(cuts)))
        loudness = loudness * jnp.repeat(heights, extent[axis_at] // parts).reshape([-1 if axis == axis_at else 1 for axis in range(len(extent))])
    return loudness


def normal_values(key, dims, scale, most, pieces=(), held_as=jnp.bfloat16):
    level = shard_levels(key, dims, pieces, -0.22, 0.18) if pieces else 1.0
    values = jax.random.normal(key, dims, jnp.float32) * scale * level
    return jnp.minimum(jnp.maximum(values, -most), most).astype(held_as)


def setup_inputs(seed: int = 0) -> dict:
    streams_of = jax.random.split(jax.random.key(seed), 11)
    return {
        "start_disp": normal_values(streams_of[0], (SLABS, 3, RAD, NA, CIR), 0.05, 0.2, ((0, 16), (3, 2)), jnp.float32),
        "start_vel": normal_values(streams_of[1], (SLABS, 3, RAD, NA, CIR), 0.05, 0.2, ((0, 16), (3, 2)), jnp.float32),
        "start_visc": normal_values(streams_of[2], (SLABS, 3, RAD, NA, CIR), 0.05, 0.2, ((0, 16), (3, 2)), jnp.float32),
        "init_state": normal_values(streams_of[3], (3, 3, RAD, NA, CIR), 0.05, 0.2, ((3, 2),), jnp.float32),
        "inv_mass": jnp.clip(jnp.exp(math.log(1.0) - 1.0498221 * jax.random.uniform(streams_of[4], (RAD, NA, CIR), jnp.float32) ** shard_levels(streams_of[4], (RAD, NA, CIR), ((1, 2),), -0.2, 0.2)), 0.35, 1.0),
        "damping_rate": jnp.clip(jnp.exp(math.log(0.2) - 4.6051702 * jax.random.uniform(streams_of[5], (RAD, NA, CIR), jnp.float32) ** shard_levels(streams_of[5], (RAD, NA, CIR), ((1, 2),), -0.2, 0.2)), 0.002, 0.2),
        "visc_rate": jnp.clip(jnp.exp(math.log(2.0) - 4.6051702 * jax.random.uniform(streams_of[6], (RAD, NA, CIR), jnp.float32) ** shard_levels(streams_of[6], (RAD, NA, CIR), ((1, 2),), -0.2, 0.2)), 0.02, 2.0),
        "fiber_stiff": jnp.clip(jnp.exp(math.log(0.25) - 1.609438 * jax.random.uniform(streams_of[7], (RAD, NA, CIR), jnp.float32) ** shard_levels(streams_of[7], (RAD, NA, CIR), ((1, 2),), -0.2, 0.2)), 0.05, 0.25),
        "fiber_family": touch_ends(jax.random.randint(streams_of[8], (NA // BLK_AX, CIR // BLK_CIR), 0, 4), jax.random.fold_in(streams_of[8], 1), 0, 3).astype(jnp.int32),
        "pressure": jnp.clip(jnp.exp(math.log(1.0) - 1.609438 * jax.random.uniform(streams_of[9], (SLABS, STEPS), jnp.float32) ** shard_levels(streams_of[9], (SLABS, STEPS), ((0, 16),), -0.2, 0.2)), 0.2, 1.0),
    }


COEF_AXIAL = 0.22
COEF_CIRC = 0.22
COEF_RADIAL = 0.12
VISC_SHARE = 0.6
TIME_STEP = 1.0
FIBER_ANGLES = (0.5, -0.5, 0.9, -0.9)


def directions(fiber_family, block_rows, block_cols):
    count_a, count_c = fiber_family.shape
    spread = jnp.broadcast_to(fiber_family[:, None, :, None], (count_a, block_rows, count_c, block_cols))
    spread = spread.reshape(count_a * block_rows, count_c * block_cols)
    cosine = jnp.zeros(spread.shape, jnp.float32)
    sine_part = jnp.zeros(spread.shape, jnp.float32)
    for family, radians in enumerate(FIBER_ANGLES):
        chosen = jnp.where(spread == family, 1.0, 0.0).astype(jnp.float32)
        cosine = cosine + chosen * math.cos(radians)
        sine_part = sine_part + chosen * math.sin(radians)
    return cosine, sine_part


def materials(fiber_stiff, fiber_family):
    cosine, sine_part = directions(fiber_family, BLK_AX, BLK_CIR)
    return jnp.stack([fiber_stiff, jnp.broadcast_to(cosine, fiber_stiff.shape), jnp.broadcast_to(sine_part, fiber_stiff.shape)])


def pad_axial(field):
    return jnp.pad(field, ((0, 0), (0, 0), (1, 1), (0, 0)))


def stencil(u_pad, mat_pad):
    center = u_pad[:, :, 1:-1]
    axial = u_pad[:, :, 2:] + u_pad[:, :, :-2] - 2.0 * center
    circle = jnp.roll(center, 1, 3) + jnp.roll(center, -1, 3) - 2.0 * center
    radial_pad = jnp.pad(center, ((0, 0), (1, 1), (0, 0), (0, 0)))
    radial = radial_pad[:, 2:] + radial_pad[:, :-2] - 2.0 * center
    elastic = COEF_AXIAL * axial + COEF_CIRC * circle + COEF_RADIAL * radial
    grad_axial = u_pad[:, :, 1:] - u_pad[:, :, :-1]
    lower = u_pad[:, :, :-1]
    grad_circ = jnp.roll(lower, -1, 3) - lower
    stiffness = mat_pad[0, :, :-1]
    cosine = mat_pad[1, :, :-1]
    sine_part = mat_pad[2, :, :-1]
    strain = cosine * cosine * grad_axial[1] + sine_part * sine_part * grad_circ[2] + cosine * sine_part * (grad_axial[2] + grad_circ[1])
    weight = jnp.exp(strain * strain)
    sigma = stiffness * weight * strain
    axial_one = sigma * cosine * cosine
    mixed = sigma * cosine * sine_part
    circ_two = sigma * sine_part * sine_part
    own_mixed = mixed[:, 1:]
    own_circ = circ_two[:, 1:]
    force_one = (axial_one[:, 1:] - axial_one[:, :-1]) + (own_mixed - jnp.roll(own_mixed, 1, 2))
    force_two = (mixed[:, 1:] - mixed[:, :-1]) + (own_circ - jnp.roll(own_circ, 1, 2))
    fiber = jnp.stack([jnp.zeros_like(force_one), force_one, force_two])
    return elastic + fiber, elastic, weight[:, 1:]


def fine_step(state, u_pad, mat_pad, inv_mass, damping_rate, decay_factor, pressure_now):
    displace, velocity, viscous = state
    force_total, elastic, weight = stencil(u_pad, mat_pad)
    inner_wall = jnp.zeros((3, displace.shape[1], 1, 1), jnp.float32).at[0, 0].set(1.0)
    load_total = force_total + viscous + pressure_now * inner_wall
    acceleration = inv_mass * load_total - damping_rate * velocity
    next_vel = velocity + TIME_STEP * acceleration
    next_disp = displace + TIME_STEP * next_vel
    next_visc = decay_factor * viscous + (1.0 - decay_factor) * VISC_SHARE * elastic
    return (next_disp, next_vel, next_visc), weight


def coarse_matrix(inv_mass, damping_rate, fiber_stiff, weight):
    half_step = 0.5 * STEPS * TIME_STEP
    stiffness = inv_mass * (2.0 * (COEF_AXIAL + COEF_CIRC + COEF_RADIAL) + 2.0 * fiber_stiff * weight)
    damping_part = half_step * damping_rate
    square_part = half_step * half_step * stiffness
    determinant = 1.0 + damping_part + square_part
    return jnp.stack([(1.0 + damping_part - square_part) / determinant, (2.0 * half_step) / determinant, -2.0 * half_step * stiffness / determinant, (1.0 - damping_part - square_part) / determinant])


def relax(start, mat_pad, inv_mass, damping_rate, decay_factor, fiber_stiff, pressure_row, pad_field):
    state = start
    first_weight = None
    for section in range(STEPS):
        u_pad = pad_field(state[0])
        state, weight = fine_step(state, u_pad, mat_pad, inv_mass, damping_rate, decay_factor, pressure_row[section])
        if section == 0:
            first_weight = weight
    return state, coarse_matrix(inv_mass, damping_rate, fiber_stiff, first_weight)


def reference(start_disp, start_vel, start_visc, init_state, inv_mass, damping_rate, visc_rate, fiber_stiff, fiber_family, pressure):
    mat_pad = pad_axial(materials(fiber_stiff, fiber_family))
    decay_factor = jnp.exp(-TIME_STEP * visc_rate)

    def one_slab(slab):
        displace, velocity, viscous, pressure_row = slab
        state, gmat = relax((displace, velocity, viscous), mat_pad, inv_mass, damping_rate, decay_factor, fiber_stiff, pressure_row, pad_axial)
        return state[0], state[1], state[2], gmat

    end_disp, end_vel, end_visc, gmats = lax.map(one_slab, (start_disp, start_vel, start_visc, pressure))
    prior_disp = jnp.concatenate([init_state[0][None], end_disp[:-1]], 0)
    prior_vel = jnp.concatenate([init_state[1][None], end_vel[:-1]], 0)
    prior_visc = jnp.concatenate([init_state[2][None], end_visc[:-1]], 0)
    resid_disp = prior_disp - start_disp
    resid_vel = prior_vel - start_vel

    def chain(carried, inputs):
        error_disp, error_vel = carried
        gmat, part_disp, part_vel = inputs
        sum_disp = error_disp + part_disp
        sum_vel = error_vel + part_vel
        next_disp = gmat[0] * sum_disp + gmat[1] * sum_vel
        next_vel = gmat[2] * sum_disp + gmat[3] * sum_vel
        return (next_disp, next_vel), (error_disp, error_vel)

    zero_field = jnp.zeros(start_disp.shape[1:], jnp.float32)
    _, (errors_disp, errors_vel) = lax.scan(chain, (zero_field, zero_field), (gmats, resid_disp, resid_vel))
    return prior_disp + errors_disp, prior_vel + errors_vel, prior_visc
```

```python
import functools
import math

import jax
import jax.numpy as jnp
from jax import lax
from jax.experimental import pallas as pl
from jax.experimental.pallas import tpu as pltpu
from jax.sharding import PartitionSpec as P

STEPS = 4
BLK_AX = 4
BLK_CIR = 32
COEF_AXIAL = 0.22
COEF_CIRC = 0.22
COEF_RADIAL = 0.12
VISC_SHARE = 0.6
TIME_STEP = 1.0
FIBER_ANGLES = (0.5, -0.5, 0.9, -0.9)
CORES = 2
HALO = STEPS
F32 = jnp.float32
VMEM_LIMIT = 24 * 1024 * 1024


def call(kernel, out_shape, operands, scratch=(), any_space=(), smem=()):
    specs = []
    for k in range(len(operands)):
        if k in any_space:
            specs.append(pl.BlockSpec(memory_space=pl.ANY))
        elif k in smem:
            specs.append(pl.BlockSpec(memory_space=pltpu.SMEM))
        else:
            specs.append(pl.BlockSpec(memory_space=pltpu.VMEM))
    return pl.pallas_call(
        kernel,
        out_shape=out_shape,
        in_specs=specs,
        out_specs=jax.tree.map(lambda _: pl.BlockSpec(memory_space=pltpu.VMEM), out_shape),
        scratch_shapes=list(scratch),
        compiler_params=pltpu.CompilerParams(vmem_limit_bytes=VMEM_LIMIT),
    )(*operands)


def shape(*dims):
    return jax.ShapeDtypeStruct(dims, F32)


def iota(dims, axis):
    return lax.broadcasted_iota(jnp.int32, dims, axis)


def direction_tile(family_ref, first, second, cols):
    row = iota((8, cols), 0)
    block = iota((8, cols), 1) // BLK_CIR
    family = jnp.zeros((8, cols), jnp.int32)
    for k in range(cols // BLK_CIR):
        index = jnp.where(row < BLK_AX, family_ref[first, k], family_ref[second, k])
        family = jnp.where(block == k, index, family)
    cosine = jnp.zeros((8, cols), F32)
    sine = jnp.zeros((8, cols), F32)
    for index, angle in enumerate(FIBER_ANGLES):
        cosine = jnp.where(family == index, math.cos(angle), cosine)
        sine = jnp.where(family == index, math.sin(angle), sine)
    return cosine, sine


def pack_kernel(sides, *refs):
    fields, family_ref = refs[:7], refs[7]
    outs = refs[8 : 8 + len(sides)]
    states = refs[8 + len(sides)]
    statics = refs[9 + len(sides)]
    sem = refs[10 + len(sides)]
    rows, cols = fields[0].shape[-2:]
    block_rows = family_ref.shape[0]
    place = lax.axis_index("space")
    for out_ref, side in zip(outs, sides):
        tail = (place == 0) if side == "inner" else (side == "tail")
        start = jnp.where(tail, rows - 8, 0) if side == "inner" else (rows - 8 if tail else 0)
        if side == "inner":
            start = pl.multiple_of(start, 8)
        copies = []
        for k in range(3):
            copies.append(
                pltpu.make_async_copy(
                    fields[k].at[0, :, :, pl.ds(start, 8), :], states.at[k], sem.at[k]
                )
            )
        for k in range(4):
            copies.append(
                pltpu.make_async_copy(
                    fields[3 + k].at[:, pl.ds(start, 8), :], statics.at[k], sem.at[3 + k]
                )
            )
        for copy in copies:
            copy.start()
        end_block = jnp.where(tail, block_rows - 1, 0) if side == "inner" else (block_rows - 1 if tail else 0)
        cosine, sine = direction_tile(family_ref, end_block, end_block, cols)
        low = iota((8, cols), 0) < HALO
        for copy in copies:
            copy.wait()

        def pair(first, second):
            up = pltpu.roll(first, 4, 0)
            down = pltpu.roll(second, 4, 0)
            return jnp.where(tail, jnp.where(low, up, second), jnp.where(low, first, down))

        at = 0
        for k in range(3):
            for comp in range(3):
                for layer in range(0, 4, 2):
                    out_ref[at] = pair(states[k, comp, layer], states[k, comp, layer + 1])
                    at += 1
        for k in range(4):
            for layer in range(0, 4, 2):
                out_ref[at] = pair(statics[k, layer], statics[k, layer + 1])
                at += 1
        out_ref[at] = jnp.where(low, cosine, sine)


def coarse(inv_mass, damping, stiff, weight):
    half_step = 0.5 * STEPS * TIME_STEP
    k = inv_mass * (2.0 * (COEF_AXIAL + COEF_CIRC + COEF_RADIAL) + 2.0 * stiff * weight)
    damp = half_step * damping
    square = half_step * half_step * k
    scale = 1.0 / (1.0 + damp + square)
    return (
        (1.0 + damp - square) * scale,
        (2.0 * half_step) * scale,
        (-2.0 * half_step) * k * scale,
        (1.0 - damp - square) * scale,
    )


def relax_kernel(
    disp_ref, vel_ref, visc_ref, mass_ref, damp_ref, rate_ref, stiff_ref, family_ref, pressure_ref,
    next_ref, prev_ref, keep_ref, send_ref, end_visc_ref,
    u_s, v_s, q_s, mass_s, damp_s, decay_s, share_s, stiff_s, cc_s, cs_s, ss_s, w_s,
):
    rows, cols = disp_ref.shape[-2:]
    total = rows + 8
    layers = disp_ref.shape[2]
    place = lax.axis_index("space")
    has_next = place < lax.axis_size("space") - 1
    has_prev = place > 0
    low = iota((8, cols), 0) < HALO
    live = jnp.where(low, has_next.astype(jnp.int32), has_prev.astype(jnp.int32)) > 0

    def halo(at):
        after, before = next_ref[at], prev_ref[at]
        first = jnp.where(live, jnp.where(low, after, pltpu.roll(before, 4, 0)), 0.0)
        second = jnp.where(live, jnp.where(low, pltpu.roll(after, 4, 0), before), 0.0)
        return first, second

    at = 0
    for source, target in ((disp_ref, u_s.at[0]), (vel_ref, v_s), (visc_ref, q_s)):
        for comp in range(3):
            for layer in range(0, layers, 2):
                pair = halo(at)
                at += 1
                for j in range(2):
                    target[comp * layers + layer + j, 0:rows, :] = source[0, comp, layer + j]
                    target[comp * layers + layer + j, rows:total, :] = pair[j]
    for source, target in ((mass_ref, mass_s), (damp_ref, damp_s), (rate_ref, decay_s), (stiff_ref, stiff_s)):
        for layer in range(0, layers, 2):
            pair = halo(at)
            at += 1
            for j in range(2):
                target[layer + j, 0:rows, :] = source[layer + j]
                target[layer + j, rows:total, :] = pair[j]
    for layer in range(layers):
        decay = jnp.exp(-TIME_STEP * decay_s[layer])
        decay_s[layer] = decay
        share_s[layer] = (1.0 - decay) * VISC_SHARE
    for tile in range(rows // 8):
        cosine, sine = direction_tile(family_ref, 2 * tile, 2 * tile + 1, cols)
        cc_s[8 * tile : 8 * tile + 8, :] = cosine * cosine
        cs_s[8 * tile : 8 * tile + 8, :] = cosine * sine
        ss_s[8 * tile : 8 * tile + 8, :] = sine * sine
    cosine, sine = halo(at)
    cc_s[rows:total, :] = cosine * cosine
    cs_s[rows:total, :] = cosine * sine
    ss_s[rows:total, :] = sine * sine

    def succ(a):
        return pltpu.roll(a, total - 1, 0)

    def pred(a):
        return pltpu.roll(a, 1, 0)

    def right(a):
        return pltpu.roll(a, cols - 1, 1)

    def left(a):
        return pltpu.roll(a, 1, 1)

    def step(s, carry):
        now = lax.rem(s, 2)
        later = 1 - now
        load = pressure_ref[0, s]
        for layer in range(layers):
            mass, damp = mass_s[layer], damp_s[layer]
            decay, share = decay_s[layer], share_s[layer]
            cc, cs, ss = cc_s[...], cs_s[...], ss_s[...]
            u = [u_s[now, comp * layers + layer] for comp in range(3)]
            ahead = [succ(a) for a in u]
            beside = [right(a) for a in u]
            strain = (
                cc * (ahead[1] - u[1])
                + ss * (beside[2] - u[2])
                + cs * ((ahead[2] - u[2]) + (beside[1] - u[1]))
            )
            weight = jnp.exp(strain * strain)
            w_s[s, layer] = weight
            sigma = stiff_s[layer] * weight * strain
            axial_one, mixed, circ_two = cc * sigma, cs * sigma, ss * sigma
            fiber = [
                None,
                (axial_one - pred(axial_one)) + (mixed - left(mixed)),
                (mixed - pred(mixed)) + (circ_two - left(circ_two)),
            ]
            for comp in range(3):
                k = comp * layers + layer
                elastic = COEF_AXIAL * ((ahead[comp] + pred(u[comp])) + (beside[comp] + left(u[comp])))
                if layer == 0:
                    radial = u_s[now, k + 1]
                elif layer == layers - 1:
                    radial = u_s[now, k - 1]
                else:
                    radial = u_s[now, k - 1] + u_s[now, k + 1]
                elastic = (elastic + COEF_RADIAL * radial) - (
                    2.0 * (COEF_AXIAL + COEF_CIRC + COEF_RADIAL)
                ) * u[comp]
                visc = q_s[k]
                force = elastic + visc
                if fiber[comp] is not None:
                    force = force + fiber[comp]
                elif layer == 0:
                    force = force + load
                vel = v_s[k]
                vel = vel + (mass * force - damp * vel)
                v_s[k] = vel
                u_s[later, k] = u[comp] + vel
                q_s[k] = decay * visc + share * elastic
        return carry

    lax.fori_loop(0, STEPS, step, 0)

    core = lax.rem(lax.axis_index("tm"), CORES)
    half = layers // CORES
    for layer in range(layers):
        weight = w_s[0, layer, 0:rows, :]
        g = coarse(mass_s[layer, 0:rows, :], damp_s[layer, 0:rows, :], stiff_s[layer, 0:rows, :], weight)
        mine = core == layer // half
        pieces = [weight]
        for comp in range(3):
            k = comp * layers + layer
            pieces.append(
                u_s[STEPS % 2, k, 0:rows, :] - (g[0] * disp_ref[0, comp, layer] + g[1] * vel_ref[0, comp, layer])
            )
        for comp in range(3):
            k = comp * layers + layer
            pieces.append(
                v_s[k, 0:rows, :] - (g[2] * disp_ref[0, comp, layer] + g[3] * vel_ref[0, comp, layer])
            )

        @pl.when(mine)
        def _():
            for k, piece in enumerate(pieces):
                keep_ref[k, layer % half] = piece

        @pl.when(jnp.logical_not(mine))
        def _():
            for k, piece in enumerate(pieces):
                send_ref[k, layer % half] = piece

        for comp in range(3):
            end_visc_ref[comp, layer] = q_s[comp * layers + layer, 0:rows, :]


def layout(group, half, rows):
    part_rows = half * rows // group
    return part_rows, rows // part_rows


def compose_kernel(group, keep_ref, got_ref, mass_ref, damp_ref, stiff_ref, *outs):
    half, rows, cols = keep_ref.shape[1:]
    part_rows, per_layer = layout(group, half, rows)
    index = lax.axis_index("tm")
    core = lax.rem(index, CORES)
    place = lax.rem(index // CORES, group)
    first_core = core == 0
    for m in range(group):
        part = jnp.bitwise_xor(place, m)
        layer = part // per_layer
        start = pl.multiple_of(lax.rem(part, per_layer) * part_rows, 8)
        own_layer = core * half + layer
        cut = pl.ds(start, part_rows)
        keep = [keep_ref[k, layer, cut, :] for k in range(7)]
        got = [got_ref[k, layer, cut, :] for k in range(7)]
        early = [jnp.where(first_core, a, b) for a, b in zip(keep, got)]
        late = [jnp.where(first_core, b, a) for a, b in zip(keep, got)]
        g = coarse(mass_ref[own_layer, cut, :], damp_ref[own_layer, cut, :], stiff_ref[own_layer, cut, :], late[0])
        outs[m][0] = early[0]
        outs[m][1] = late[0]
        for comp in range(3):
            a, b = early[1 + comp], early[4 + comp]
            outs[m][2 + comp] = (g[0] * a + g[1] * b) + late[1 + comp]
            outs[m][5 + comp] = (g[2] * a + g[3] * b) + late[4 + comp]


def chain(group, maps, mass, damp, stiff, state, visit):
    place = lax.rem(lax.axis_index("tm") // CORES, group)
    for s in range(group):
        visit(s, state)
        one = maps[s]
        first = coarse(mass, damp, stiff, one[0])
        second = coarse(mass, damp, stiff, one[1])
        new = [None] * 6
        for comp in range(3):
            a, b = state[comp], state[3 + comp]
            a, b = first[0] * a + first[1] * b, first[2] * a + first[3] * b
            new[comp] = (second[0] * a + second[1] * b) + one[2 + comp]
            new[3 + comp] = (second[2] * a + second[3] * b) + one[5 + comp]
        state = new
    return state


def own_cut(group, half, rows):
    part_rows, per_layer = layout(group, half, rows)
    index = lax.axis_index("tm")
    core = lax.rem(index, CORES)
    place = lax.rem(index // CORES, group)
    layer = core * half + place // per_layer
    start = pl.multiple_of(lax.rem(place, per_layer) * part_rows, 8)
    return place, layer, pl.ds(start, part_rows)


def lower_kernel(group, half, *refs):
    parts = refs[:group]
    mass_ref, damp_ref, stiff_ref, init_ref, out_ref, maps = refs[group:]
    rows = mass_ref.shape[-2]
    place, layer, cut = own_cut(group, half, rows)
    for m in range(group):
        maps[jnp.bitwise_xor(place, m)] = parts[m][...]
    state = [init_ref[k // 3, k % 3, layer, cut, :] for k in range(6)]
    state = chain(
        group, maps, mass_ref[layer, cut, :], damp_ref[layer, cut, :], stiff_ref[layer, cut, :], state,
        lambda s, state: None,
    )
    for k in range(6):
        out_ref[k] = state[k]


def upper_kernel(group, half, *refs):
    parts = refs[:group]
    mass_ref, damp_ref, stiff_ref, init_ref, hop_ref = refs[group : group + 5]
    outs = refs[group + 5 : 2 * group + 5]
    maps, found = refs[2 * group + 5 :]
    rows = mass_ref.shape[-2]
    place, layer, cut = own_cut(group, half, rows)
    lower = lax.axis_index("tm") < CORES * group
    for m in range(group):
        maps[jnp.bitwise_xor(place, m)] = parts[m][...]
    state = [jnp.where(lower, init_ref[k // 3, k % 3, layer, cut, :], hop_ref[k]) for k in range(6)]

    def visit(s, state):
        for k in range(6):
            found[s, k] = state[k]

    chain(
        group, maps, mass_ref[layer, cut, :], damp_ref[layer, cut, :], stiff_ref[layer, cut, :], state, visit
    )
    for m in range(group):
        outs[m][...] = found[jnp.bitwise_xor(place, m)]


def spread_kernel(group, *refs):
    parts = refs[:group]
    keep_ref, got_ref, mass_ref, damp_ref, stiff_ref, mine_ref, send_ref = refs[group:]
    half, rows, cols = keep_ref.shape[1:]
    part_rows, per_layer = layout(group, half, rows)
    index = lax.axis_index("tm")
    core = lax.rem(index, CORES)
    place = lax.rem(index // CORES, group)
    first_core = core == 0
    for m in range(group):
        part = jnp.bitwise_xor(place, m)
        layer = part // per_layer
        start = pl.multiple_of(lax.rem(part, per_layer) * part_rows, 8)
        own_layer = core * half + layer
        cut = pl.ds(start, part_rows)
        early = [jnp.where(first_core, keep_ref[k, layer, cut, :], got_ref[k, layer, cut, :]) for k in range(7)]
        g = coarse(mass_ref[own_layer, cut, :], damp_ref[own_layer, cut, :], stiff_ref[own_layer, cut, :], early[0])
        for comp in range(3):
            a, b = parts[m][comp], parts[m][3 + comp]
            next_a = (g[0] * a + g[1] * b) + early[1 + comp]
            next_b = (g[2] * a + g[3] * b) + early[4 + comp]
            mine_ref[comp, layer, cut, :] = jnp.where(first_core, a, next_a)
            mine_ref[3 + comp, layer, cut, :] = jnp.where(first_core, b, next_b)
            send_ref[comp, layer, cut, :] = jnp.where(first_core, next_a, a)
            send_ref[3 + comp, layer, cut, :] = jnp.where(first_core, next_b, b)


def join_kernel(mine_ref, got_ref, disp_ref, vel_ref):
    half = mine_ref.shape[1]
    core = lax.rem(lax.axis_index("tm"), CORES)
    for comp in range(3):
        for layer in range(half):
            disp_ref[0, comp, core * half + layer] = mine_ref[comp, layer]
            disp_ref[0, comp, (1 - core) * half + layer] = got_ref[comp, layer]
            vel_ref[0, comp, core * half + layer] = mine_ref[3 + comp, layer]
            vel_ref[0, comp, (1 - core) * half + layer] = got_ref[3 + comp, layer]


def swap_cores(value):
    count = lax.axis_size("tm")
    return lax.ppermute(value, "tm", [(i, i ^ 1) for i in range(count)])


def transpose_parts(parts):
    count = lax.axis_size("tm")
    done = [parts[0]]
    for m in range(1, len(parts)):
        done.append(lax.ppermute(parts[m], "tm", [(i, i ^ (CORES * m)) for i in range(count)]))
    return done


def shards(
    start_disp, start_vel, start_visc, init_state, inv_mass, damping_rate, visc_rate, fiber_stiff,
    fiber_family, pressure,
):
    slabs, spaces = lax.axis_size("tm"), lax.axis_size("space")
    group = slabs // CORES // 2
    layers, rows, cols = inv_mass.shape
    half = layers // CORES
    total = rows + 8
    part_rows, _ = layout(group, half, rows)

    tiles = (9 * layers + 4 * layers + 2) // 2
    packed = shape(tiles, 8, cols)
    sides = ("inner",) if spaces == 2 else ("tail", "head")
    packs = call(
        functools.partial(pack_kernel, sides),
        [packed] * len(sides),
        (start_disp, start_vel, start_visc, inv_mass, damping_rate, visc_rate, fiber_stiff, fiber_family),
        [
            pltpu.VMEM((3, 3, layers, 8, cols), F32),
            pltpu.VMEM((4, layers, 8, cols), F32),
            pltpu.SemaphoreType.DMA((7,)),
        ],
        any_space=range(7),
        smem=(7,),
    )
    if spaces == 2:
        after = before = lax.ppermute(packs[0], "space", [(0, 1), (1, 0)])
    else:
        before = lax.ppermute(packs[0], "space", [(i, i + 1) for i in range(spaces - 1)])
        after = lax.ppermute(packs[1], "space", [(i + 1, i) for i in range(spaces - 1)])

    keep, send, end_visc = call(
        relax_kernel,
        [shape(7, half, rows, cols), shape(7, half, rows, cols), shape(3, layers, rows, cols)],
        (
            start_disp, start_vel, start_visc, inv_mass, damping_rate, visc_rate, fiber_stiff, fiber_family,
            pressure, after, before,
        ),
        [
            pltpu.VMEM((2, 3 * layers, total, cols), F32),
            pltpu.VMEM((3 * layers, total, cols), F32),
            pltpu.VMEM((3 * layers, total, cols), F32),
        ]
        + [pltpu.VMEM((layers, total, cols), F32)] * 5
        + [pltpu.VMEM((total, cols), F32)] * 3
        + [pltpu.VMEM((STEPS, layers, total, cols), F32)],
        smem=(7, 8),
    )
    got = swap_cores(send)
    visc = lax.ppermute(end_visc, "tm", [(i, i + 1) for i in range(slabs - 1)])

    parts = call(
        functools.partial(compose_kernel, group),
        [shape(8, part_rows, cols)] * group,
        (keep, got, inv_mass, damping_rate, fiber_stiff),
    )
    parts = transpose_parts(parts)
    maps = pltpu.VMEM((group, 8, part_rows, cols), F32)
    edge = call(
        functools.partial(lower_kernel, group, half),
        shape(6, part_rows, cols),
        (*parts, inv_mass, damping_rate, fiber_stiff, init_state),
        [maps],
    )
    hop = lax.ppermute(edge, "tm", [(i, i + slabs // 2) for i in range(slabs // 2)])
    states = call(
        functools.partial(upper_kernel, group, half),
        [shape(6, part_rows, cols)] * group,
        (*parts, inv_mass, damping_rate, fiber_stiff, init_state, hop),
        [maps, pltpu.VMEM((group, 6, part_rows, cols), F32)],
    )
    states = transpose_parts(states)
    mine, other = call(
        functools.partial(spread_kernel, group),
        [shape(6, half, rows, cols)] * 2,
        (*states, keep, got, inv_mass, damping_rate, fiber_stiff),
    )
    other = swap_cores(other)
    field = shape(1, 3, layers, rows, cols)
    new_disp, new_vel = call(join_kernel, [field, field], (mine, other))
    first_slab = lax.axis_index("tm") == 0
    new_visc = jnp.where(first_slab, init_state[2], visc)[None]
    return new_disp, new_vel, new_visc


def solution(mesh):
    slab = P("tm", None, None, "space", None)
    cell = P(None, "space", None)
    return jax.shard_map(
        shards,
        mesh=mesh,
        in_specs=(
            slab, slab, slab, P(None, None, None, "space", None), cell, cell, cell, cell,
            P("space", None), P("tm", None),
        ),
        out_specs=(slab, slab, slab),
        check_vma=False,
    )
```

```python
import functools
import math

import jax
import jax.numpy as jnp
from jax import lax
from jax.experimental import pallas as pl
from jax.experimental.pallas import tpu as pltpu
from jax.sharding import PartitionSpec as P

STEPS = 4
BLK_AX = 4
BLK_CIR = 32
COEF_AXIAL = 0.22
COEF_CIRC = 0.22
COEF_RADIAL = 0.12
VISC_SHARE = 0.6
TIME_STEP = 1.0
FIBER_ANGLES = (0.5, -0.5, 0.9, -0.9)
CORES = 2
HALO = STEPS
F32 = jnp.float32
VMEM_LIMIT = 24 * 1024 * 1024


def call(kernel, out_shape, operands, scratch=(), in_hbm=(), aliases={}):
    specs = []
    for k in range(len(operands)):
        specs.append(pl.BlockSpec(memory_space=pltpu.HBM if k in in_hbm else pltpu.VMEM))
    return pl.pallas_call(
        kernel,
        out_shape=out_shape,
        in_specs=specs,
        out_specs=jax.tree.map(lambda _: pl.BlockSpec(memory_space=pltpu.VMEM), out_shape),
        scratch_shapes=list(scratch),
        compiler_params=pltpu.CompilerParams(vmem_limit_bytes=VMEM_LIMIT),
        input_output_aliases=aliases,
    )(*operands)


def shape(*dims):
    return jax.ShapeDtypeStruct(dims, F32)


def iota(dims, axis):
    return lax.broadcasted_iota(jnp.int32, dims, axis)


def low_rows(cols):
    return iota((8, cols), 0) < HALO


def rolled_tile(load, tile, tiles, cols):
    last = (tile + tiles - 1) % tiles if isinstance(tile, int) else lax.rem(tile + tiles - 1, tiles)
    return jnp.where(low_rows(cols), pltpu.roll(load(last), 4, 0), pltpu.roll(load(tile), 4, 0))


def direction_tile(family_ref, first, second, cols):
    block = iota((8, cols), 1) // BLK_CIR
    family = jnp.zeros((8, cols), jnp.int32)
    for k in range(cols // BLK_CIR):
        index = jnp.where(low_rows(cols), family_ref[first, k], family_ref[second, k])
        family = jnp.where(block == k, index, family)
    cosine = jnp.zeros((8, cols), F32)
    sine = jnp.zeros((8, cols), F32)
    for index, angle in enumerate(FIBER_ANGLES):
        cosine = jnp.where(family == index, math.cos(angle), cosine)
        sine = jnp.where(family == index, math.sin(angle), sine)
    return cosine, sine


def pack_kernel(sides, *refs):
    fields, family_ref = refs[:7], refs[7]
    outs = refs[8 : 8 + len(sides)]
    states, statics, family_s, sem = refs[8 + len(sides) :]
    rows, cols = fields[0].shape[-2:]
    block_rows = family_ref.shape[0]
    place = lax.axis_index("space")
    directions = pltpu.make_async_copy(family_ref, family_s, sem.at[7])
    for n, (out_ref, side) in enumerate(zip(outs, sides)):
        tail = (place == 0) if side == "facing" else jnp.bool_(side == "tail")
        start = pl.multiple_of(jnp.where(tail, rows - 8, 0), 8)
        copies = [] if n else [directions]
        for k in range(3):
            source = fields[k].at[0, :, :, pl.ds(start, 8), :]
            copies.append(pltpu.make_async_copy(source, states.at[k], sem.at[k]))
        for k in range(4):
            source = fields[3 + k].at[:, pl.ds(start, 8), :]
            copies.append(pltpu.make_async_copy(source, statics.at[k], sem.at[3 + k]))
        for copy in copies:
            copy.start()
        for copy in copies:
            copy.wait()
        low = low_rows(cols)

        def pair(first, second):
            up = pltpu.roll(first, 4, 0)
            down = pltpu.roll(second, 4, 0)
            return jnp.where(tail, jnp.where(low, up, second), jnp.where(low, first, down))

        at = 0
        for k in range(3):
            for comp in range(3):
                for layer in range(0, 4, 2):
                    out_ref[at] = pair(states[k, comp, layer], states[k, comp, layer + 1])
                    at += 1
        for k in range(4):
            for layer in range(0, 4, 2):
                out_ref[at] = pair(statics[k, layer], statics[k, layer + 1])
                at += 1
        end_block = jnp.where(tail, block_rows - 1, 0)
        cosine, sine = direction_tile(family_s, end_block, end_block, cols)
        out_ref[at] = jnp.where(low, cosine, sine)


def coarse(inv_mass, damping, stiff, weight):
    half_step = 0.5 * STEPS * TIME_STEP
    k = inv_mass * (2.0 * (COEF_AXIAL + COEF_CIRC + COEF_RADIAL) + 2.0 * stiff * weight)
    damp = half_step * damping
    square = half_step * half_step * k
    scale = 1.0 / (1.0 + damp + square)
    return (
        (1.0 + damp - square) * scale,
        (2.0 * half_step) * scale,
        (-2.0 * half_step) * k * scale,
        (1.0 - damp - square) * scale,
    )


class Window:
    def __init__(self, refs):
        self.u, self.v, self.q, self.sigma, self.weight, self.static, self.dirs, self.load = refs
        self.steps, _, self.layers, self.tiles, _, self.cols = self.u.shape

    @staticmethod
    def shapes(layers, tiles, cols):
        return (
            [(STEPS + 1, 3, layers, tiles, 8, cols)] * 3
            + [(STEPS, layers, tiles, 8, cols)] * 2
            + [(MASS_TO_SHARE, layers, tiles, 8, cols)]
            + [(9, tiles, 8, cols), (STEPS, 8, cols)]
        )


MASS, DAMP, RATE, STIFF, DECAY, SHARE, MASS_TO_SHARE = range(7)


def pred(a, before):
    return jnp.where(iota(a.shape, 0) == 0, pltpu.roll(before, 1, 0), pltpu.roll(a, 1, 0))


def succ(a, after):
    return jnp.where(iota(a.shape, 0) == 7, pltpu.roll(after, 7, 0), pltpu.roll(a, 7, 0))


def right(a):
    return pltpu.roll(a, a.shape[1] - 1, 1)


def left(a):
    return pltpu.roll(a, 1, 1)


def prepare(win, before_dirs):
    pairs = []
    for tile in range(win.tiles):
        cosine, sine = win.dirs[0, tile], win.dirs[1, tile]
        pairs.append((cosine * cosine, cosine * sine, sine * sine))
    for tile in range(win.tiles):
        cc, cs, ss = pairs[tile]
        before = before_dirs(tile, pairs)
        values = (cc, cs, ss, cc + cs, cs + ss, pred(cc, before[0]), pred(cs, before[1]), left(cs), left(ss))
        for k, value in enumerate(values):
            win.dirs[k, tile] = value
        for layer in range(win.layers):
            decay = jnp.exp(-TIME_STEP * win.static[RATE, layer, tile])
            win.static[DECAY, layer, tile] = decay
            win.static[SHARE, layer, tile] = (1.0 - decay) * VISC_SHARE


def fine_steps(win, order, before, after, before_sigma):
    def step(s, carry):
        def neighbours(layer, tile):
            u = [win.u[s, comp, layer, tile] for comp in range(3)]
            ahead = [succ(u[comp], after(s, comp, layer, tile)) for comp in range(3)]
            return u, ahead, [right(a) for a in u]

        def stress(layer, tile, u, ahead, beside):
            strain = (
                win.dirs[0, tile] * (ahead[1] - u[1])
                + win.dirs[2, tile] * (beside[2] - u[2])
                + win.dirs[1, tile] * ((ahead[2] - u[2]) + (beside[1] - u[1]))
            )
            weight = jnp.exp(strain * strain)
            sigma = win.static[STIFF, layer, tile] * weight * strain
            win.sigma[s, layer, tile] = sigma
            win.weight[s, layer, tile] = weight
            return sigma

        for layer in range(win.layers):
            known = {}
            if before_sigma is None:
                known[order[-1]] = stress(layer, order[-1], *neighbours(layer, order[-1]))
            for n, tile in enumerate(order):
                u, ahead, beside = neighbours(layer, tile)
                if tile not in known:
                    known[tile] = stress(layer, tile, u, ahead, beside)
                sigma = known[tile]
                last = known[order[n - 1]] if before_sigma is None else before_sigma(s, layer, tile, sigma)
                sigma_pred, sigma_left = pred(sigma, last), left(sigma)
                behind = [pred(u[comp], before(s, comp, layer, tile)) for comp in range(3)]
                fiber = [None] + [
                    win.dirs[3 + k, tile] * sigma
                    - win.dirs[5 + k, tile] * sigma_pred
                    - win.dirs[7 + k, tile] * sigma_left
                    for k in range(2)
                ]
                for comp in range(3):
                    around = (ahead[comp] + behind[comp]) + (beside[comp] + left(u[comp]))
                    if layer == 0:
                        radial = win.u[s, comp, layer + 1, tile]
                    elif layer == win.layers - 1:
                        radial = win.u[s, comp, layer - 1, tile]
                    else:
                        radial = win.u[s, comp, layer - 1, tile] + win.u[s, comp, layer + 1, tile]
                    elastic = (COEF_AXIAL * around + COEF_RADIAL * radial) - (
                        2.0 * (COEF_AXIAL + COEF_CIRC + COEF_RADIAL)
                    ) * u[comp]
                    visc = win.q[s, comp, layer, tile]
                    force = elastic + visc
                    if fiber[comp] is not None:
                        force = force + fiber[comp]
                    elif layer == 0:
                        force = force + win.load[s]
                    vel = win.v[s, comp, layer, tile]
                    vel = vel + (win.static[MASS, layer, tile] * force - win.static[DAMP, layer, tile] * vel)
                    win.v[s + 1, comp, layer, tile] = vel
                    win.u[s + 1, comp, layer, tile] = u[comp] + vel
                    win.q[s + 1, comp, layer, tile] = (
                        win.static[DECAY, layer, tile] * visc + win.static[SHARE, layer, tile] * elastic
                    )
        return carry

    lax.fori_loop(0, STEPS, step, 0)


def put_maps(win, tiles, end, keep_ref, send_ref, end_visc_ref):
    core = lax.rem(lax.axis_index("tm"), CORES)
    half = win.layers // CORES
    for layer in range(win.layers):
        for tile in tiles:
            weight = end(lambda w: w.weight.at[0], layer, tile)
            g = coarse(win.static[MASS, layer, tile], win.static[DAMP, layer, tile], win.static[STIFF, layer, tile], weight)
            pieces = [weight]
            start = [(win.u[0, comp, layer, tile], win.v[0, comp, layer, tile]) for comp in range(3)]
            for comp, (disp, vel) in enumerate(start):
                pieces.append(end(lambda w: w.u.at[STEPS, comp], layer, tile) - (g[0] * disp + g[1] * vel))
            for comp, (disp, vel) in enumerate(start):
                pieces.append(end(lambda w: w.v.at[STEPS, comp], layer, tile) - (g[2] * disp + g[3] * vel))
            to = (layer % half) * win.tiles + tile

            @pl.when(core == layer // half)
            def _():
                for k, piece in enumerate(pieces):
                    keep_ref[k, to] = piece

            @pl.when(core != layer // half)
            def _():
                for k, piece in enumerate(pieces):
                    send_ref[k, to] = piece

            for comp in range(3):
                end_visc_ref[comp, layer, tile] = end(lambda w: w.q.at[STEPS, comp], layer, tile)


def inner_kernel(*refs):
    fields, family_ref, pressure_ref, outs = refs[:7], refs[7], refs[8], refs[9:12]
    win = Window(refs[12:20])
    facing_ref = refs[20]
    states, statics, family_s, pressure_s, sem = refs[21:]
    tiles, cols, layers = win.tiles, win.cols, win.layers
    blocks = family_ref.shape[0]
    copies = []
    for k in range(3):
        copies.append(pltpu.make_async_copy(fields[k].at[0], states.at[k], sem.at[k]))
    for k in range(4):
        copies.append(pltpu.make_async_copy(fields[3 + k], statics.at[k], sem.at[3 + k]))
    directions = pltpu.make_async_copy(family_ref, family_s, sem.at[7])
    loads = pltpu.make_async_copy(pressure_ref, pressure_s, sem.at[8])
    for copy in (directions, loads, *copies):
        copy.start()
    directions.wait()
    loads.wait()
    for tile in range(tiles):
        win.dirs[0, tile], win.dirs[1, tile] = direction_tile(
            family_s, (2 * tile + blocks - 1) % blocks, 2 * tile, cols
        )
    facing_ref[0], facing_ref[1] = win.dirs[0, 0], win.dirs[1, 0]
    for s in range(STEPS):
        win.load[s] = jnp.full((8, cols), pressure_s[0, s], F32)

    def rolled(source, target):
        rows = [pltpu.roll(source[8 * tile : 8 * tile + 8, :], 4, 0) for tile in range(tiles)]
        for tile in range(tiles):
            target[tile] = jnp.where(low_rows(cols), rows[tile - 1], rows[tile])

    for k, target in enumerate((win.u, win.v, win.q)):
        copies[k].wait()
        for comp in range(3):
            for layer in range(layers):
                rolled(states.at[k, comp, layer], target.at[0, comp, layer])
    for k in range(4):
        copies[3 + k].wait()
        for layer in range(layers):
            rolled(statics.at[k, layer], win.static.at[k, layer])
    prepare(win, lambda tile, pairs: pairs[tile - 1])
    fine_steps(
        win, [*range(1, tiles), 0],
        lambda s, comp, layer, tile: win.u[s, comp, layer, (tile + tiles - 1) % tiles],
        lambda s, comp, layer, tile: win.u[s, comp, layer, (tile + 1) % tiles],
        None,
    )
    put_maps(win, range(1, tiles), lambda of, layer, tile: of(win)[layer, tile], *outs)


def outer_kernel(*refs):
    next_ref, prev_ref = refs[:2]
    inner = Window(refs[2:10])
    facing_ref = refs[13]
    outs = refs[14:17]
    win = Window(refs[17:])
    layers, cols = win.layers, win.cols
    place = lax.axis_index("space")
    has_next = place < lax.axis_size("space") - 1
    has_prev = place > 0
    low = low_rows(cols)
    live = jnp.where(low, has_prev.astype(jnp.int32), has_next.astype(jnp.int32)) > 0

    def halo(at, own, target):
        after, before = next_ref[at], prev_ref[at]
        for j in range(2):
            ahead = pltpu.roll(after, 4, 0) if j == 0 else after
            behind = before if j == 0 else pltpu.roll(before, 4, 0)
            target(j)[0] = jnp.where(low, own(j), jnp.where(live, ahead, 0.0))
            target(j)[1] = jnp.where(low, jnp.where(live, behind, 0.0), own(j))

    at = 0
    for source, target in ((inner.u, win.u), (inner.v, win.v), (inner.q, win.q)):
        for comp in range(3):
            for layer in range(0, layers, 2):
                halo(at, lambda j: source[0, comp, layer + j, 0], lambda j: target.at[0, comp, layer + j])
                at += 1
    for k in (MASS, DAMP, RATE, STIFF):
        for layer in range(0, layers, 2):
            halo(at, lambda j: inner.static[k, layer + j, 0], lambda j: win.static.at[k, layer + j])
            at += 1
    halo(at, lambda j: facing_ref[j], lambda j: win.dirs.at[j])
    for s in range(STEPS):
        win.load[s] = inner.load[s]
    last = inner.tiles - 1
    prepare(win, lambda tile, pairs: (inner.dirs[0, last], inner.dirs[1, last]))
    fine_steps(
        win, [0, 1],
        lambda s, comp, layer, tile: inner.u[s, comp, layer, last],
        lambda s, comp, layer, tile: inner.u[s, comp, layer, 1],
        lambda s, layer, tile, own: inner.sigma[s, layer, last],
    )

    def end(of, layer, tile):
        return jnp.where(low, of(win)[layer, 0], of(win)[layer, 1])

    put_maps(inner, [0], end, *outs)


class Cut:
    def __init__(self, group, half, tiles, cols):
        self.group, self.half, self.tiles, self.cols = group, half, tiles, cols
        self.count = half * tiles
        self.size = self.count // group

    def of(self, part):
        first = part * self.size
        core = lax.rem(lax.axis_index("tm"), CORES)
        return first, core * self.half + first // self.tiles, lax.rem(first, self.tiles)

    def place(self):
        return lax.rem(lax.axis_index("tm") // CORES, self.group)


def part_coarse(static_ref, layer, tile, weight):
    return coarse(static_ref[MASS, layer, tile], static_ref[DAMP, layer, tile], static_ref[STIFF, layer, tile], weight)


def compose_kernel(cut, keep_ref, got_ref, static_ref, *outs):
    first_core = lax.rem(lax.axis_index("tm"), CORES) == 0
    for m in range(cut.group):
        first, layer, tile = cut.of(jnp.bitwise_xor(cut.place(), m))
        for i in range(cut.size):
            keep = [keep_ref[k, first + i] for k in range(7)]
            got = [got_ref[k, first + i] for k in range(7)]
            early = [jnp.where(first_core, a, b) for a, b in zip(keep, got)]
            late = [jnp.where(first_core, b, a) for a, b in zip(keep, got)]
            g = part_coarse(static_ref, layer, tile + i, late[0])
            outs[m][0, i] = early[0]
            outs[m][1, i] = late[0]
            for comp in range(3):
                a, b = early[1 + comp], early[4 + comp]
                outs[m][2 + comp, i] = (g[0] * a + g[1] * b) + late[1 + comp]
                outs[m][5 + comp, i] = (g[2] * a + g[3] * b) + late[4 + comp]


def chain(cut, parts, maps, static_ref, start, visit):
    place = cut.place()
    _, layer, tile = cut.of(place)
    for m in range(cut.group):
        maps[jnp.bitwise_xor(place, m)] = parts[m][...]
    for i in range(cut.size):
        state = [start(k, layer, tile + i, i) for k in range(6)]
        for s in range(cut.group):
            visit(s, i, state)
            first = part_coarse(static_ref, layer, tile + i, maps[s, 0, i])
            second = part_coarse(static_ref, layer, tile + i, maps[s, 1, i])
            new = [None] * 6
            for comp in range(3):
                a, b = state[comp], state[3 + comp]
                a, b = first[0] * a + first[1] * b, first[2] * a + first[3] * b
                new[comp] = (second[0] * a + second[1] * b) + maps[s, 2 + comp, i]
                new[3 + comp] = (second[2] * a + second[3] * b) + maps[s, 5 + comp, i]
            state = new
        visit(cut.group, i, state)


def first_state(cut, init_ref):
    def start(k, layer, tile, i):
        def load(t):
            return init_ref[k // 3, k % 3, layer, pl.ds(pl.multiple_of(8 * t, 8), 8), :]

        return rolled_tile(load, tile, cut.tiles, cut.cols)

    return start


def lower_kernel(cut, *refs):
    parts = refs[: cut.group]
    static_ref, init_ref, out_ref, maps = refs[cut.group :]

    def visit(s, i, state):
        if s == cut.group:
            for k in range(6):
                out_ref[k, i] = state[k]

    chain(cut, parts, maps, static_ref, first_state(cut, init_ref), visit)


def upper_kernel(cut, *refs):
    parts = refs[: cut.group]
    static_ref, init_ref, hop_ref = refs[cut.group : cut.group + 3]
    outs = refs[cut.group + 3 : 2 * cut.group + 3]
    maps, found = refs[2 * cut.group + 3 :]
    lower = lax.axis_index("tm") < CORES * cut.group
    first = first_state(cut, init_ref)

    def start(k, layer, tile, i):
        return jnp.where(lower, first(k, layer, tile, i), hop_ref[k, i])

    def visit(s, i, state):
        if s < cut.group:
            for k in range(6):
                found[s, k, i] = state[k]

    chain(cut, parts, maps, static_ref, start, visit)
    for m in range(cut.group):
        outs[m][...] = found[jnp.bitwise_xor(cut.place(), m)]


def spread_kernel(cut, *refs):
    parts = refs[: cut.group]
    keep_ref, got_ref, static_ref, mine_ref, send_ref = refs[cut.group :]
    first_core = lax.rem(lax.axis_index("tm"), CORES) == 0
    for m in range(cut.group):
        first, layer, tile = cut.of(jnp.bitwise_xor(cut.place(), m))
        for i in range(cut.size):
            early = [jnp.where(first_core, keep_ref[k, first + i], got_ref[k, first + i]) for k in range(7)]
            g = part_coarse(static_ref, layer, tile + i, early[0])
            for comp in range(3):
                a, b = parts[m][comp, i], parts[m][3 + comp, i]
                next_a = (g[0] * a + g[1] * b) + early[1 + comp]
                next_b = (g[2] * a + g[3] * b) + early[4 + comp]
                mine_ref[comp, first + i] = jnp.where(first_core, a, next_a)
                mine_ref[3 + comp, first + i] = jnp.where(first_core, b, next_b)
                send_ref[comp, first + i] = jnp.where(first_core, next_a, a)
                send_ref[3 + comp, first + i] = jnp.where(first_core, next_b, b)


def unroll(load, store, tiles, cols):
    rows = [pltpu.roll(load(tile), 4, 0) for tile in range(tiles)]
    for tile in range(tiles):
        store(slice(8 * tile, 8 * tile + 8), jnp.where(low_rows(cols), rows[tile], rows[(tile + 1) % tiles]))


def join_kernel(cut, mine_ref, got_ref, disp_ref, vel_ref):
    core = lax.rem(lax.axis_index("tm"), CORES)
    for k in range(6):
        for layer in range(cut.half):
            for source, own in ((mine_ref, core), (got_ref, 1 - core)):
                def store(rows, value):
                    (disp_ref, vel_ref)[k // 3][0, k % 3, own * cut.half + layer, rows, :] = value

                unroll(lambda tile: source[k, layer * cut.tiles + tile], store, cut.tiles, cut.cols)


def visc_kernel(cut, visc_ref, init_ref, out_ref):
    first_slab = lax.axis_index("tm") == 0
    for comp in range(3):
        for layer in range(visc_ref.shape[1]):
            def store(rows, value):
                out_ref[0, comp, layer, rows, :] = jnp.where(first_slab, init_ref[2, comp, layer, rows, :], value)

            unroll(lambda tile: visc_ref[comp, layer, tile], store, cut.tiles, cut.cols)


def swap_cores(value):
    count = lax.axis_size("tm")
    return lax.ppermute(value, "tm", [(i, i ^ 1) for i in range(count)])


def transpose_parts(parts):
    count = lax.axis_size("tm")
    done = [parts[0]]
    for m in range(1, len(parts)):
        done.append(lax.ppermute(parts[m], "tm", [(i, i ^ (CORES * m)) for i in range(count)]))
    return done


def shards(
    start_disp, start_vel, start_visc, init_state, inv_mass, damping_rate, visc_rate, fiber_stiff,
    fiber_family, pressure,
):
    slabs, spaces = lax.axis_size("tm"), lax.axis_size("space")
    group = slabs // CORES // 2
    layers, rows, cols = inv_mass.shape
    half, tiles = layers // CORES, rows // 8
    cut = Cut(group, half, tiles, cols)

    packed = shape((9 * layers + 4 * layers + 2) // 2, 8, cols)
    sides = ("facing",) if spaces == 2 else ("tail", "head")
    in_hbm = [
        pltpu.with_memory_space_constraint(x, pltpu.HBM)
        for x in (
            start_disp, start_vel, start_visc, inv_mass, damping_rate, visc_rate, fiber_stiff, fiber_family, pressure
        )
    ]
    packs = call(
        functools.partial(pack_kernel, sides),
        [packed] * len(sides),
        in_hbm[:8],
        [
            pltpu.VMEM((3, 3, layers, 8, cols), F32),
            pltpu.VMEM((4, layers, 8, cols), F32),
            pltpu.SMEM(fiber_family.shape, jnp.int32),
            pltpu.SemaphoreType.DMA((8,)),
        ],
        in_hbm=range(8),
    )
    if spaces == 2:
        after = before = lax.ppermute(packs[0], "space", [(0, 1), (1, 0)])
    else:
        before = lax.ppermute(packs[0], "space", [(i, i + 1) for i in range(spaces - 1)])
        after = lax.ppermute(packs[1], "space", [(i + 1, i) for i in range(spaces - 1)])

    map_shape = shape(7, cut.count, 8, cols)
    outs = [map_shape, map_shape, shape(3, layers, tiles, 8, cols)]
    held = [shape(*dims) for dims in Window.shapes(layers, tiles, cols)]
    partial = call(
        inner_kernel,
        outs + held + [shape(2, 8, cols)],
        in_hbm,
        [
            pltpu.VMEM((3, 3, layers, rows, cols), F32),
            pltpu.VMEM((4, layers, rows, cols), F32),
            pltpu.SMEM(fiber_family.shape, jnp.int32),
            pltpu.SMEM(pressure.shape, F32),
            pltpu.SemaphoreType.DMA((9,)),
        ],
        in_hbm=range(9),
    )
    ends, held, facing = partial[:3], partial[3:11], partial[11]
    keep, send, end_visc = call(
        outer_kernel,
        outs,
        (after, before, *held, *ends, facing),
        [pltpu.VMEM(dims, F32) for dims in Window.shapes(layers, 2, cols)],
        aliases={10: 0, 11: 1, 12: 2},
    )
    static = held[5]
    got = swap_cores(send)
    visc = lax.ppermute(end_visc, "tm", [(i, i + 1) for i in range(slabs - 1)])

    parts = call(
        functools.partial(compose_kernel, cut), [shape(8, cut.size, 8, cols)] * group, (keep, got, static)
    )
    parts = transpose_parts(parts)
    maps = pltpu.VMEM((group, 8, cut.size, 8, cols), F32)
    edge = call(
        functools.partial(lower_kernel, cut), shape(6, cut.size, 8, cols), (*parts, static, init_state), [maps]
    )
    hop = lax.ppermute(edge, "tm", [(i, i + slabs // 2) for i in range(slabs // 2)])
    states = call(
        functools.partial(upper_kernel, cut),
        [shape(6, cut.size, 8, cols)] * group,
        (*parts, static, init_state, hop),
        [maps, pltpu.VMEM((group, 6, cut.size, 8, cols), F32)],
    )
    states = transpose_parts(states)
    mine, other = call(
        functools.partial(spread_kernel, cut), [shape(6, cut.count, 8, cols)] * 2, (*states, keep, got, static)
    )
    other = swap_cores(other)
    field = shape(1, 3, layers, rows, cols)
    new_disp, new_vel = call(functools.partial(join_kernel, cut), [field, field], (mine, other))
    new_visc = call(functools.partial(visc_kernel, cut), field, (visc, init_state))
    return new_disp, new_vel, new_visc


def solution(mesh):
    slab = P("tm", None, None, "space", None)
    cell = P(None, "space", None)
    return jax.shard_map(
        shards,
        mesh=mesh,
        in_specs=(
            slab, slab, slab, P(None, None, None, "space", None), cell, cell, cell, cell,
            P("space", None), P("tm", None),
        ),
        out_specs=(slab, slab, slab),
        check_vma=False,
    )
```

```python
import functools
import math

import jax
import jax.numpy as jnp
from jax import lax
from jax.experimental import pallas as pl
from jax.experimental.pallas import tpu as pltpu
from jax.sharding import PartitionSpec as P

STEPS = 4
BLK_AX = 4
BLK_CIR = 32
COEF_AXIAL = 0.22
COEF_CIRC = 0.22
COEF_RADIAL = 0.12
VISC_SHARE = 0.6
TIME_STEP = 1.0
FIBER_ANGLES = (0.5, -0.5, 0.9, -0.9)
CORES = 2
HALO = STEPS
F32 = jnp.float32
VMEM_LIMIT = 24 * 1024 * 1024


def call(kernel, out_shape, operands, scratch=(), in_hbm=(), out_hbm=False, aliases={}):
    specs = []
    for k in range(len(operands)):
        specs.append(pl.BlockSpec(memory_space=pltpu.HBM if k in in_hbm else pltpu.VMEM))
    return pl.pallas_call(
        kernel,
        out_shape=out_shape,
        in_specs=specs,
        out_specs=jax.tree.map(lambda _: pl.BlockSpec(memory_space=pltpu.HBM if out_hbm else pltpu.VMEM), out_shape),
        scratch_shapes=list(scratch),
        compiler_params=pltpu.CompilerParams(vmem_limit_bytes=VMEM_LIMIT),
        input_output_aliases=aliases,
    )(*operands)


def shape(*dims):
    return jax.ShapeDtypeStruct(dims, F32)


def iota(dims, axis):
    return lax.broadcasted_iota(jnp.int32, dims, axis)


def low_rows(cols):
    return iota((8, cols), 0) < HALO


def rolled_tile(load, tile, tiles, cols):
    last = (tile + tiles - 1) % tiles if isinstance(tile, int) else lax.rem(tile + tiles - 1, tiles)
    return jnp.where(low_rows(cols), pltpu.roll(load(last), 4, 0), pltpu.roll(load(tile), 4, 0))


def direction_tile(family_ref, first, second, cols):
    block = iota((8, cols), 1) // BLK_CIR
    family = jnp.zeros((8, cols), jnp.int32)
    for k in range(cols // BLK_CIR):
        index = jnp.where(low_rows(cols), family_ref[first, k], family_ref[second, k])
        family = jnp.where(block == k, index, family)
    cosine = jnp.zeros((8, cols), F32)
    sine = jnp.zeros((8, cols), F32)
    for index, angle in enumerate(FIBER_ANGLES):
        cosine = jnp.where(family == index, math.cos(angle), cosine)
        sine = jnp.where(family == index, math.sin(angle), sine)
    return cosine, sine


def pack_kernel(sides, *refs):
    fields, family_ref = refs[:7], refs[7]
    outs = refs[8 : 8 + len(sides)]
    states, statics, family_s, sem = refs[8 + len(sides) :]
    rows, cols = fields[0].shape[-2:]
    block_rows = family_ref.shape[0]
    place = lax.axis_index("space")
    directions = pltpu.make_async_copy(family_ref, family_s, sem.at[7])
    for n, (out_ref, side) in enumerate(zip(outs, sides)):
        tail = (place == 0) if side == "facing" else jnp.bool_(side == "tail")
        start = pl.multiple_of(jnp.where(tail, rows - 8, 0), 8)
        copies = [] if n else [directions]
        for k in range(3):
            source = fields[k].at[0, :, :, pl.ds(start, 8), :]
            copies.append(pltpu.make_async_copy(source, states.at[k], sem.at[k]))
        for k in range(4):
            source = fields[3 + k].at[:, pl.ds(start, 8), :]
            copies.append(pltpu.make_async_copy(source, statics.at[k], sem.at[3 + k]))
        for copy in copies:
            copy.start()
        for copy in copies:
            copy.wait()
        low = low_rows(cols)

        def pair(first, second):
            up = pltpu.roll(first, 4, 0)
            down = pltpu.roll(second, 4, 0)
            return jnp.where(tail, jnp.where(low, up, second), jnp.where(low, first, down))

        at = 0
        for k in range(3):
            for comp in range(3):
                for layer in range(0, 4, 2):
                    out_ref[at] = pair(states[k, comp, layer], states[k, comp, layer + 1])
                    at += 1
        for k in range(4):
            for layer in range(0, 4, 2):
                out_ref[at] = pair(statics[k, layer], statics[k, layer + 1])
                at += 1
        end_block = jnp.where(tail, block_rows - 1, 0)
        cosine, sine = direction_tile(family_s, end_block, end_block, cols)
        out_ref[at] = jnp.where(low, cosine, sine)


def coarse(inv_mass, damping, stiff, weight):
    half_step = 0.5 * STEPS * TIME_STEP
    k = inv_mass * (2.0 * (COEF_AXIAL + COEF_CIRC + COEF_RADIAL) + 2.0 * stiff * weight)
    damp = half_step * damping
    square = half_step * half_step * k
    scale = 1.0 / (1.0 + damp + square)
    return (
        (1.0 + damp - square) * scale,
        (2.0 * half_step) * scale,
        (-2.0 * half_step) * k * scale,
        (1.0 - damp - square) * scale,
    )


class Window:
    def __init__(self, refs):
        self.u, self.v, self.q, self.sigma, self.weight, self.static, self.dirs, self.load = refs
        self.steps, _, self.layers, self.tiles, _, self.cols = self.u.shape

    @staticmethod
    def shapes(layers, tiles, cols):
        return (
            [(STEPS + 1, 3, layers, tiles, 8, cols)] * 3
            + [(STEPS, layers, tiles, 8, cols)] * 2
            + [(MASS_TO_SHARE, layers, tiles, 8, cols)]
            + [(9, tiles, 8, cols), (STEPS, 8, cols)]
        )


MASS, DAMP, RATE, STIFF, DECAY, SHARE, MASS_TO_SHARE = range(7)


def pred(a, before):
    return jnp.where(iota(a.shape, 0) == 0, pltpu.roll(before, 1, 0), pltpu.roll(a, 1, 0))


def succ(a, after):
    return jnp.where(iota(a.shape, 0) == 7, pltpu.roll(after, 7, 0), pltpu.roll(a, 7, 0))


def right(a):
    return pltpu.roll(a, a.shape[1] - 1, 1)


def left(a):
    return pltpu.roll(a, 1, 1)


def prepare(win, before_dirs):
    pairs = []
    for tile in range(win.tiles):
        cosine, sine = win.dirs[0, tile], win.dirs[1, tile]
        pairs.append((cosine * cosine, cosine * sine, sine * sine))
    for tile in range(win.tiles):
        cc, cs, ss = pairs[tile]
        before = before_dirs(tile, pairs)
        values = (cc, cs, ss, cc + cs, cs + ss, pred(cc, before[0]), pred(cs, before[1]), left(cs), left(ss))
        for k, value in enumerate(values):
            win.dirs[k, tile] = value
        for layer in range(win.layers):
            decay = jnp.exp(-TIME_STEP * win.static[RATE, layer, tile])
            win.static[DECAY, layer, tile] = decay
            win.static[SHARE, layer, tile] = (1.0 - decay) * VISC_SHARE


def fine_steps(win, order, before, after, before_sigma):
    def step(s, carry):
        def neighbours(layer, tile):
            u = [win.u[s, comp, layer, tile] for comp in range(3)]
            ahead = [succ(u[comp], after(s, comp, layer, tile)) for comp in range(3)]
            return u, ahead, [right(a) for a in u]

        def stress(layer, tile, u, ahead, beside):
            strain = (
                win.dirs[0, tile] * (ahead[1] - u[1])
                + win.dirs[2, tile] * (beside[2] - u[2])
                + win.dirs[1, tile] * ((ahead[2] - u[2]) + (beside[1] - u[1]))
            )
            weight = jnp.exp(strain * strain)
            sigma = win.static[STIFF, layer, tile] * weight * strain
            win.sigma[s, layer, tile] = sigma
            win.weight[s, layer, tile] = weight
            return sigma

        for layer in range(win.layers):
            known = {}
            if before_sigma is None:
                known[order[-1]] = stress(layer, order[-1], *neighbours(layer, order[-1]))
            for n, tile in enumerate(order):
                u, ahead, beside = neighbours(layer, tile)
                if tile not in known:
                    known[tile] = stress(layer, tile, u, ahead, beside)
                sigma = known[tile]
                last = known[order[n - 1]] if before_sigma is None else before_sigma(s, layer, tile, sigma)
                sigma_pred, sigma_left = pred(sigma, last), left(sigma)
                behind = [pred(u[comp], before(s, comp, layer, tile)) for comp in range(3)]
                fiber = [None] + [
                    win.dirs[3 + k, tile] * sigma
                    - win.dirs[5 + k, tile] * sigma_pred
                    - win.dirs[7 + k, tile] * sigma_left
                    for k in range(2)
                ]
                for comp in range(3):
                    around = (ahead[comp] + behind[comp]) + (beside[comp] + left(u[comp]))
                    if layer == 0:
                        radial = win.u[s, comp, layer + 1, tile]
                    elif layer == win.layers - 1:
                        radial = win.u[s, comp, layer - 1, tile]
                    else:
                        radial = win.u[s, comp, layer - 1, tile] + win.u[s, comp, layer + 1, tile]
                    elastic = (COEF_AXIAL * around + COEF_RADIAL * radial) - (
                        2.0 * (COEF_AXIAL + COEF_CIRC + COEF_RADIAL)
                    ) * u[comp]
                    visc = win.q[s, comp, layer, tile]
                    force = elastic + visc
                    if fiber[comp] is not None:
                        force = force + fiber[comp]
                    elif layer == 0:
                        force = force + win.load[s]
                    vel = win.v[s, comp, layer, tile]
                    vel = vel + (win.static[MASS, layer, tile] * force - win.static[DAMP, layer, tile] * vel)
                    win.v[s + 1, comp, layer, tile] = vel
                    win.u[s + 1, comp, layer, tile] = u[comp] + vel
                    win.q[s + 1, comp, layer, tile] = (
                        win.static[DECAY, layer, tile] * visc + win.static[SHARE, layer, tile] * elastic
                    )
        return carry

    lax.fori_loop(0, STEPS, step, 0)


def put_maps(win, tiles, end, keep_ref, send_ref, end_visc_ref):
    core = lax.rem(lax.axis_index("tm"), CORES)
    half = win.layers // CORES
    for layer in range(win.layers):
        for tile in tiles:
            weight = end(lambda w: w.weight.at[0], layer, tile)
            g = coarse(win.static[MASS, layer, tile], win.static[DAMP, layer, tile], win.static[STIFF, layer, tile], weight)
            pieces = [weight]
            start = [(win.u[0, comp, layer, tile], win.v[0, comp, layer, tile]) for comp in range(3)]
            for comp, (disp, vel) in enumerate(start):
                pieces.append(end(lambda w: w.u.at[STEPS, comp], layer, tile) - (g[0] * disp + g[1] * vel))
            for comp, (disp, vel) in enumerate(start):
                pieces.append(end(lambda w: w.v.at[STEPS, comp], layer, tile) - (g[2] * disp + g[3] * vel))
            to = (layer % half) * win.tiles + tile

            @pl.when(core == layer // half)
            def _():
                for k, piece in enumerate(pieces):
                    keep_ref[k, to] = piece

            @pl.when(core != layer // half)
            def _():
                for k, piece in enumerate(pieces):
                    send_ref[k, to] = piece

            for comp in range(3):
                end_visc_ref[comp, layer, tile] = end(lambda w: w.q.at[STEPS, comp], layer, tile)


def inner_kernel(*refs):
    fields, family_ref, pressure_ref, outs = refs[:7], refs[7], refs[8], refs[9:12]
    win = Window(refs[12:20])
    facing_ref = refs[20]
    states, statics, family_s, pressure_s, sem = refs[21:]
    tiles, cols, layers = win.tiles, win.cols, win.layers
    blocks = family_ref.shape[0]
    copies = []
    for k in range(3):
        copies.append(pltpu.make_async_copy(fields[k].at[0], states.at[k], sem.at[k]))
    for k in range(4):
        copies.append(pltpu.make_async_copy(fields[3 + k], statics.at[k], sem.at[3 + k]))
    directions = pltpu.make_async_copy(family_ref, family_s, sem.at[7])
    loads = pltpu.make_async_copy(pressure_ref, pressure_s, sem.at[8])
    for copy in (directions, loads, *copies):
        copy.start()
    directions.wait()
    loads.wait()
    for tile in range(tiles):
        win.dirs[0, tile], win.dirs[1, tile] = direction_tile(
            family_s, (2 * tile + blocks - 1) % blocks, 2 * tile, cols
        )
    facing_ref[0], facing_ref[1] = win.dirs[0, 0], win.dirs[1, 0]
    for s in range(STEPS):
        win.load[s] = jnp.full((8, cols), pressure_s[0, s], F32)

    def rolled(source, target):
        rows = [pltpu.roll(source[8 * tile : 8 * tile + 8, :], 4, 0) for tile in range(tiles)]
        for tile in range(tiles):
            target[tile] = jnp.where(low_rows(cols), rows[tile - 1], rows[tile])

    for k, target in enumerate((win.u, win.v, win.q)):
        copies[k].wait()
        for comp in range(3):
            for layer in range(layers):
                rolled(states.at[k, comp, layer], target.at[0, comp, layer])
    for k in range(4):
        copies[3 + k].wait()
        for layer in range(layers):
            rolled(statics.at[k, layer], win.static.at[k, layer])
    prepare(win, lambda tile, pairs: pairs[tile - 1])
    fine_steps(
        win, [*range(1, tiles), 0],
        lambda s, comp, layer, tile: win.u[s, comp, layer, (tile + tiles - 1) % tiles],
        lambda s, comp, layer, tile: win.u[s, comp, layer, (tile + 1) % tiles],
        None,
    )
    put_maps(win, range(1, tiles), lambda of, layer, tile: of(win)[layer, tile], *outs)


def outer_kernel(*refs):
    next_ref, prev_ref = refs[:2]
    inner = Window(refs[2:10])
    facing_ref = refs[13]
    outs = refs[14:17]
    win = Window(refs[17:])
    layers, cols = win.layers, win.cols
    place = lax.axis_index("space")
    has_next = place < lax.axis_size("space") - 1
    has_prev = place > 0
    low = low_rows(cols)
    live = jnp.where(low, has_prev.astype(jnp.int32), has_next.astype(jnp.int32)) > 0

    def halo(at, own, target):
        after, before = next_ref[at], prev_ref[at]
        for j in range(2):
            ahead = pltpu.roll(after, 4, 0) if j == 0 else after
            behind = before if j == 0 else pltpu.roll(before, 4, 0)
            target(j)[0] = jnp.where(low, own(j), jnp.where(live, ahead, 0.0))
            target(j)[1] = jnp.where(low, jnp.where(live, behind, 0.0), own(j))

    at = 0
    for source, target in ((inner.u, win.u), (inner.v, win.v), (inner.q, win.q)):
        for comp in range(3):
            for layer in range(0, layers, 2):
                halo(at, lambda j: source[0, comp, layer + j, 0], lambda j: target.at[0, comp, layer + j])
                at += 1
    for k in (MASS, DAMP, RATE, STIFF):
        for layer in range(0, layers, 2):
            halo(at, lambda j: inner.static[k, layer + j, 0], lambda j: win.static.at[k, layer + j])
            at += 1
    halo(at, lambda j: facing_ref[j], lambda j: win.dirs.at[j])
    for s in range(STEPS):
        win.load[s] = inner.load[s]
    last = inner.tiles - 1
    prepare(win, lambda tile, pairs: (inner.dirs[0, last], inner.dirs[1, last]))
    fine_steps(
        win, [0, 1],
        lambda s, comp, layer, tile: inner.u[s, comp, layer, last],
        lambda s, comp, layer, tile: inner.u[s, comp, layer, 1],
        lambda s, layer, tile, own: inner.sigma[s, layer, last],
    )

    def end(of, layer, tile):
        return jnp.where(low, of(win)[layer, 0], of(win)[layer, 1])

    put_maps(inner, [0], end, *outs)


class Cut:
    def __init__(self, group, half, tiles, cols):
        self.group, self.half, self.tiles, self.cols = group, half, tiles, cols
        self.count = half * tiles
        self.size = self.count // group

    def of(self, part):
        first = part * self.size
        core = lax.rem(lax.axis_index("tm"), CORES)
        return first, core * self.half + first // self.tiles, lax.rem(first, self.tiles)

    def place(self):
        return lax.rem(lax.axis_index("tm") // CORES, self.group)


def part_coarse(static_ref, layer, tile, weight):
    return coarse(static_ref[MASS, layer, tile], static_ref[DAMP, layer, tile], static_ref[STIFF, layer, tile], weight)


def compose_kernel(cut, keep_ref, got_ref, static_ref, *outs):
    first_core = lax.rem(lax.axis_index("tm"), CORES) == 0
    for m in range(cut.group):
        first, layer, tile = cut.of(jnp.bitwise_xor(cut.place(), m))
        for i in range(cut.size):
            keep = [keep_ref[k, first + i] for k in range(7)]
            got = [got_ref[k, first + i] for k in range(7)]
            early = [jnp.where(first_core, a, b) for a, b in zip(keep, got)]
            late = [jnp.where(first_core, b, a) for a, b in zip(keep, got)]
            g = part_coarse(static_ref, layer, tile + i, late[0])
            outs[m][0, i] = early[0]
            outs[m][1, i] = late[0]
            for comp in range(3):
                a, b = early[1 + comp], early[4 + comp]
                outs[m][2 + comp, i] = (g[0] * a + g[1] * b) + late[1 + comp]
                outs[m][5 + comp, i] = (g[2] * a + g[3] * b) + late[4 + comp]


def chain(cut, parts, maps, static_ref, start, visit):
    place = cut.place()
    _, layer, tile = cut.of(place)
    for m in range(cut.group):
        maps[jnp.bitwise_xor(place, m)] = parts[m][...]
    for i in range(cut.size):
        state = [start(k, layer, tile + i, i) for k in range(6)]
        for s in range(cut.group):
            visit(s, i, state)
            first = part_coarse(static_ref, layer, tile + i, maps[s, 0, i])
            second = part_coarse(static_ref, layer, tile + i, maps[s, 1, i])
            new = [None] * 6
            for comp in range(3):
                a, b = state[comp], state[3 + comp]
                a, b = first[0] * a + first[1] * b, first[2] * a + first[3] * b
                new[comp] = (second[0] * a + second[1] * b) + maps[s, 2 + comp, i]
                new[3 + comp] = (second[2] * a + second[3] * b) + maps[s, 5 + comp, i]
            state = new
        visit(cut.group, i, state)


def first_state(cut, init_ref):
    def start(k, layer, tile, i):
        def load(t):
            return init_ref[k // 3, k % 3, layer, pl.ds(pl.multiple_of(8 * t, 8), 8), :]

        return rolled_tile(load, tile, cut.tiles, cut.cols)

    return start


def lower_kernel(cut, *refs):
    parts = refs[: cut.group]
    static_ref, init_ref, out_ref, maps = refs[cut.group :]

    def visit(s, i, state):
        if s == cut.group:
            for k in range(6):
                out_ref[k, i] = state[k]

    chain(cut, parts, maps, static_ref, first_state(cut, init_ref), visit)


def upper_kernel(cut, *refs):
    parts = refs[: cut.group]
    static_ref, init_ref, hop_ref = refs[cut.group : cut.group + 3]
    outs = refs[cut.group + 3 : 2 * cut.group + 3]
    maps, found = refs[2 * cut.group + 3 :]
    lower = lax.axis_index("tm") < CORES * cut.group
    first = first_state(cut, init_ref)

    def start(k, layer, tile, i):
        return jnp.where(lower, first(k, layer, tile, i), hop_ref[k, i])

    def visit(s, i, state):
        if s < cut.group:
            for k in range(6):
                found[s, k, i] = state[k]

    chain(cut, parts, maps, static_ref, start, visit)
    for m in range(cut.group):
        outs[m][...] = found[jnp.bitwise_xor(cut.place(), m)]


def spread_kernel(cut, *refs):
    parts = refs[: cut.group]
    keep_ref, got_ref, static_ref, mine_ref, send_ref = refs[cut.group :]
    first_core = lax.rem(lax.axis_index("tm"), CORES) == 0
    for m in range(cut.group):
        first, layer, tile = cut.of(jnp.bitwise_xor(cut.place(), m))
        for i in range(cut.size):
            early = [jnp.where(first_core, keep_ref[k, first + i], got_ref[k, first + i]) for k in range(7)]
            g = part_coarse(static_ref, layer, tile + i, early[0])
            for comp in range(3):
                a, b = parts[m][comp, i], parts[m][3 + comp, i]
                next_a = (g[0] * a + g[1] * b) + early[1 + comp]
                next_b = (g[2] * a + g[3] * b) + early[4 + comp]
                mine_ref[comp, first + i] = jnp.where(first_core, a, next_a)
                mine_ref[3 + comp, first + i] = jnp.where(first_core, b, next_b)
                send_ref[comp, first + i] = jnp.where(first_core, next_a, a)
                send_ref[3 + comp, first + i] = jnp.where(first_core, next_b, b)


def unroll(load, store, tiles, cols):
    rows = [pltpu.roll(load(tile), 4, 0) for tile in range(tiles)]
    for tile in range(tiles):
        store(slice(8 * tile, 8 * tile + 8), jnp.where(low_rows(cols), rows[tile], rows[(tile + 1) % tiles]))


def join_kernel(cut, other, *refs):
    part_ref, (disp_ref, vel_ref, block, sem) = refs[0], refs[-4:]
    core = lax.rem(lax.axis_index("tm"), CORES)
    place = 1 - core if other else core
    copies = []
    for k in range(6):
        for layer in range(cut.half):
            def store(rows, value):
                block[k, layer, rows, :] = value

            unroll(lambda tile: part_ref[k, layer * cut.tiles + tile], store, cut.tiles, cut.cols)
        target = (disp_ref, vel_ref)[k // 3].at[0, k % 3, pl.ds(place * cut.half, cut.half)]
        copies.append(pltpu.make_async_copy(block.at[k], target, sem.at[k]))
        copies[-1].start()
    for copy in copies:
        copy.wait()


def last_kernel(cut, other, part_ref, visc_ref, init_ref, *refs):
    disp_ref, vel_ref, out_ref, visc_s, block, sem, visc_sem = refs[-7:]
    first_slab = lax.axis_index("tm") == 0
    copies = []
    for comp in range(3):
        for layer in range(visc_ref.shape[1]):
            def store(rows, value):
                visc_s[comp, layer, rows, :] = jnp.where(first_slab, init_ref[2, comp, layer, rows, :], value)

            unroll(lambda tile: visc_ref[comp, layer, tile], store, cut.tiles, cut.cols)
        copies.append(pltpu.make_async_copy(visc_s.at[comp], out_ref.at[0, comp], visc_sem.at[comp]))
        copies[-1].start()
    join_kernel(cut, other, part_ref, disp_ref, vel_ref, block, sem)
    for copy in copies:
        copy.wait()


def swap_cores(value):
    count = lax.axis_size("tm")
    return lax.ppermute(value, "tm", [(i, i ^ 1) for i in range(count)])


def transpose_parts(parts):
    count = lax.axis_size("tm")
    done = [parts[0]]
    for m in range(1, len(parts)):
        done.append(lax.ppermute(parts[m], "tm", [(i, i ^ (CORES * m)) for i in range(count)]))
    return done


def shards(
    start_disp, start_vel, start_visc, init_state, inv_mass, damping_rate, visc_rate, fiber_stiff,
    fiber_family, pressure,
):
    slabs, spaces = lax.axis_size("tm"), lax.axis_size("space")
    group = slabs // CORES // 2
    layers, rows, cols = inv_mass.shape
    half, tiles = layers // CORES, rows // 8
    cut = Cut(group, half, tiles, cols)

    packed = shape((9 * layers + 4 * layers + 2) // 2, 8, cols)
    sides = ("facing",) if spaces == 2 else ("tail", "head")
    in_hbm = [
        pltpu.with_memory_space_constraint(x, pltpu.HBM)
        for x in (
            start_disp, start_vel, start_visc, inv_mass, damping_rate, visc_rate, fiber_stiff, fiber_family, pressure
        )
    ]
    packs = call(
        functools.partial(pack_kernel, sides),
        [packed] * len(sides),
        in_hbm[:8],
        [
            pltpu.VMEM((3, 3, layers, 8, cols), F32),
            pltpu.VMEM((4, layers, 8, cols), F32),
            pltpu.SMEM(fiber_family.shape, jnp.int32),
            pltpu.SemaphoreType.DMA((8,)),
        ],
        in_hbm=range(8),
    )
    if spaces == 2:
        after = before = lax.ppermute(packs[0], "space", [(0, 1), (1, 0)])
    else:
        before = lax.ppermute(packs[0], "space", [(i, i + 1) for i in range(spaces - 1)])
        after = lax.ppermute(packs[1], "space", [(i + 1, i) for i in range(spaces - 1)])

    map_shape = shape(7, cut.count, 8, cols)
    outs = [map_shape, map_shape, shape(3, layers, tiles, 8, cols)]
    held = [shape(*dims) for dims in Window.shapes(layers, tiles, cols)]
    partial = call(
        inner_kernel,
        outs + held + [shape(2, 8, cols)],
        in_hbm,
        [
            pltpu.VMEM((3, 3, layers, rows, cols), F32),
            pltpu.VMEM((4, layers, rows, cols), F32),
            pltpu.SMEM(fiber_family.shape, jnp.int32),
            pltpu.SMEM(pressure.shape, F32),
            pltpu.SemaphoreType.DMA((9,)),
        ],
        in_hbm=range(9),
    )
    ends, held, facing = partial[:3], partial[3:11], partial[11]
    keep, send, end_visc = call(
        outer_kernel,
        outs,
        (after, before, *held, *ends, facing),
        [pltpu.VMEM(dims, F32) for dims in Window.shapes(layers, 2, cols)],
        aliases={10: 0, 11: 1, 12: 2},
    )
    static = held[5]
    got = swap_cores(send)
    visc = lax.ppermute(end_visc, "tm", [(i, i + 1) for i in range(slabs - 1)])

    parts = call(
        functools.partial(compose_kernel, cut), [shape(8, cut.size, 8, cols)] * group, (keep, got, static)
    )
    parts = transpose_parts(parts)
    maps = pltpu.VMEM((group, 8, cut.size, 8, cols), F32)
    edge = call(
        functools.partial(lower_kernel, cut), shape(6, cut.size, 8, cols), (*parts, static, init_state), [maps]
    )
    hop = lax.ppermute(edge, "tm", [(i, i ^ (slabs // 2)) for i in range(slabs)])
    states = call(
        functools.partial(upper_kernel, cut),
        [shape(6, cut.size, 8, cols)] * group,
        (*parts, static, init_state, hop),
        [maps, pltpu.VMEM((group, 6, cut.size, 8, cols), F32)],
    )
    states = transpose_parts(states)
    mine, other = call(
        functools.partial(spread_kernel, cut), [shape(6, cut.count, 8, cols)] * 2, (*states, keep, got, static)
    )
    other = swap_cores(other)
    field = pltpu.HBM((1, 3, layers, rows, cols), F32)
    scratch = [pltpu.VMEM((6, half, rows, cols), F32), pltpu.SemaphoreType.DMA((6,))]
    joined = call(functools.partial(join_kernel, cut, False), [field, field], (mine,), scratch, out_hbm=True)
    new_disp, new_vel, new_visc = call(
        functools.partial(last_kernel, cut, True), [field] * 3, (other, visc, init_state, *joined),
        [pltpu.VMEM((3, layers, rows, cols), F32)] + scratch + [pltpu.SemaphoreType.DMA((3,))],
        in_hbm=(3, 4), out_hbm=True, aliases={3: 0, 4: 1},
    )
    return new_disp, new_vel, new_visc


def solution(mesh):
    slab = P("tm", None, None, "space", None)
    cell = P(None, "space", None)
    return jax.shard_map(
        shards,
        mesh=mesh,
        in_specs=(
            slab, slab, slab, P(None, None, None, "space", None), cell, cell, cell, cell,
            P("space", None), P("tm", None),
        ),
        out_specs=(slab, slab, slab),
        check_vma=False,
    )
```

```python
import functools
import math

import jax
import jax.numpy as jnp
from jax import lax
from jax.experimental import pallas as pl
from jax.experimental.pallas import tpu as pltpu
from jax.sharding import PartitionSpec as P

STEPS = 4
BLK_AX = 4
BLK_CIR = 32
COEF_AXIAL = 0.22
COEF_CIRC = 0.22
COEF_RADIAL = 0.12
VISC_SHARE = 0.6
TIME_STEP = 1.0
FIBER_ANGLES = (0.5, -0.5, 0.9, -0.9)
CORES = 2
HALO = STEPS
F32 = jnp.float32
VMEM_LIMIT = 24 * 1024 * 1024


def call(kernel, out_shape, operands, scratch=(), in_hbm=(), out_hbm=False, aliases={}):
    specs = []
    for k in range(len(operands)):
        specs.append(pl.BlockSpec(memory_space=pltpu.HBM if k in in_hbm else pltpu.VMEM))
    return pl.pallas_call(
        kernel,
        out_shape=out_shape,
        in_specs=specs,
        out_specs=jax.tree.map(lambda _: pl.BlockSpec(memory_space=pltpu.HBM if out_hbm else pltpu.VMEM), out_shape),
        scratch_shapes=list(scratch),
        compiler_params=pltpu.CompilerParams(vmem_limit_bytes=VMEM_LIMIT),
        input_output_aliases=aliases,
    )(*operands)


def shape(*dims):
    return jax.ShapeDtypeStruct(dims, F32)


def iota(dims, axis):
    return lax.broadcasted_iota(jnp.int32, dims, axis)


def low_rows(cols):
    return iota((8, cols), 0) < HALO


def rolled_tile(load, tile, tiles, cols):
    last = (tile + tiles - 1) % tiles if isinstance(tile, int) else lax.rem(tile + tiles - 1, tiles)
    return jnp.where(low_rows(cols), pltpu.roll(load(last), 4, 0), pltpu.roll(load(tile), 4, 0))


def own_rows(first, second):
    return jnp.where(low_rows(first.shape[1]), pltpu.roll(first, 4, 0), pltpu.roll(second, 4, 0))


def direction_tile(family_ref, first, second, cols):
    block = iota((8, cols), 1) // BLK_CIR
    family = jnp.zeros((8, cols), jnp.int32)
    for k in range(cols // BLK_CIR):
        index = jnp.where(low_rows(cols), family_ref[first, k], family_ref[second, k])
        family = jnp.where(block == k, index, family)
    cosine = jnp.zeros((8, cols), F32)
    sine = jnp.zeros((8, cols), F32)
    for index, angle in enumerate(FIBER_ANGLES):
        cosine = jnp.where(family == index, math.cos(angle), cosine)
        sine = jnp.where(family == index, math.sin(angle), sine)
    return cosine, sine


def pack_kernel(sides, *refs):
    fields, family_ref = refs[:7], refs[7]
    outs = refs[8 : 8 + len(sides)]
    states, statics, family_s, sem = refs[8 + len(sides) :]
    rows, cols = fields[0].shape[-2:]
    block_rows = family_ref.shape[0]
    place = lax.axis_index("space")
    directions = pltpu.make_async_copy(family_ref, family_s, sem.at[7])
    for n, (out_ref, side) in enumerate(zip(outs, sides)):
        tail = (place == 0) if side == "facing" else jnp.bool_(side == "tail")
        start = pl.multiple_of(jnp.where(tail, rows - 8, 0), 8)
        copies = [] if n else [directions]
        for k in range(3):
            source = fields[k].at[0, :, :, pl.ds(start, 8), :]
            copies.append(pltpu.make_async_copy(source, states.at[k], sem.at[k]))
        for k in range(4):
            source = fields[3 + k].at[:, pl.ds(start, 8), :]
            copies.append(pltpu.make_async_copy(source, statics.at[k], sem.at[3 + k]))
        for copy in copies:
            copy.start()
        for copy in copies:
            copy.wait()
        low = low_rows(cols)

        def pair(first, second):
            up = pltpu.roll(first, 4, 0)
            down = pltpu.roll(second, 4, 0)
            return jnp.where(tail, jnp.where(low, up, second), jnp.where(low, first, down))

        at = 0
        for k in range(3):
            for comp in range(3):
                for layer in range(0, 4, 2):
                    out_ref[at] = pair(states[k, comp, layer], states[k, comp, layer + 1])
                    at += 1
        for k in range(4):
            for layer in range(0, 4, 2):
                out_ref[at] = pair(statics[k, layer], statics[k, layer + 1])
                at += 1
        end_block = jnp.where(tail, block_rows - 1, 0)
        cosine, sine = direction_tile(family_s, end_block, end_block, cols)
        out_ref[at] = jnp.where(low, cosine, sine)


def coarse(inv_mass, damping, stiff, weight):
    half_step = 0.5 * STEPS * TIME_STEP
    k = inv_mass * (2.0 * (COEF_AXIAL + COEF_CIRC + COEF_RADIAL) + 2.0 * stiff * weight)
    damp = half_step * damping
    square = half_step * half_step * k
    scale = 1.0 / (1.0 + damp + square)
    return (
        (1.0 + damp - square) * scale,
        (2.0 * half_step) * scale,
        (-2.0 * half_step) * k * scale,
        (1.0 - damp - square) * scale,
    )


class Window:
    def __init__(self, refs):
        self.u, self.v, self.q, self.sigma, self.weight, self.static, self.dirs, self.load = refs
        self.steps, _, self.layers, self.tiles, _, self.cols = self.u.shape

    @staticmethod
    def shapes(layers, tiles, cols):
        return (
            [(STEPS + 1, 3, layers, tiles, 8, cols)] * 3
            + [(STEPS, layers, tiles, 8, cols)] * 2
            + [(MASS_TO_SHARE, layers, tiles, 8, cols)]
            + [(9, tiles, 8, cols), (STEPS, 8, cols)]
        )


MASS, DAMP, RATE, STIFF, DECAY, SHARE, MASS_TO_SHARE = range(7)


def pred(a, before):
    return jnp.where(iota(a.shape, 0) == 0, pltpu.roll(before, 1, 0), pltpu.roll(a, 1, 0))


def succ(a, after):
    return jnp.where(iota(a.shape, 0) == 7, pltpu.roll(after, 7, 0), pltpu.roll(a, 7, 0))


def right(a):
    return pltpu.roll(a, a.shape[1] - 1, 1)


def left(a):
    return pltpu.roll(a, 1, 1)


def prepare(win, before_dirs):
    pairs = []
    for tile in range(win.tiles):
        cosine, sine = win.dirs[0, tile], win.dirs[1, tile]
        pairs.append((cosine * cosine, cosine * sine, sine * sine))
    for tile in range(win.tiles):
        cc, cs, ss = pairs[tile]
        before = before_dirs(tile, pairs)
        values = (cc, cs, ss, cc + cs, cs + ss, pred(cc, before[0]), pred(cs, before[1]), left(cs), left(ss))
        for k, value in enumerate(values):
            win.dirs[k, tile] = value
        for layer in range(win.layers):
            decay = jnp.exp(-TIME_STEP * win.static[RATE, layer, tile])
            win.static[DECAY, layer, tile] = decay
            win.static[SHARE, layer, tile] = (1.0 - decay) * VISC_SHARE


def fine_steps(win, order, before, after, before_sigma):
    def step(s, carry):
        def neighbours(layer, tile):
            u = [win.u[s, comp, layer, tile] for comp in range(3)]
            ahead = [succ(u[comp], after(s, comp, layer, tile)) for comp in range(3)]
            return u, ahead, [right(a) for a in u]

        def stress(layer, tile, u, ahead, beside):
            strain = (
                win.dirs[0, tile] * (ahead[1] - u[1])
                + win.dirs[2, tile] * (beside[2] - u[2])
                + win.dirs[1, tile] * ((ahead[2] - u[2]) + (beside[1] - u[1]))
            )
            weight = jnp.exp(strain * strain)
            sigma = win.static[STIFF, layer, tile] * weight * strain
            win.sigma[s, layer, tile] = sigma
            win.weight[s, layer, tile] = weight
            return sigma

        for layer in range(win.layers):
            known = {}
            if before_sigma is None:
                known[order[-1]] = stress(layer, order[-1], *neighbours(layer, order[-1]))
            for n, tile in enumerate(order):
                u, ahead, beside = neighbours(layer, tile)
                if tile not in known:
                    known[tile] = stress(layer, tile, u, ahead, beside)
                sigma = known[tile]
                last = known[order[n - 1]] if before_sigma is None else before_sigma(s, layer, tile, sigma)
                sigma_pred, sigma_left = pred(sigma, last), left(sigma)
                behind = [pred(u[comp], before(s, comp, layer, tile)) for comp in range(3)]
                fiber = [None] + [
                    win.dirs[3 + k, tile] * sigma
                    - win.dirs[5 + k, tile] * sigma_pred
                    - win.dirs[7 + k, tile] * sigma_left
                    for k in range(2)
                ]
                for comp in range(3):
                    around = (ahead[comp] + behind[comp]) + (beside[comp] + left(u[comp]))
                    if layer == 0:
                        radial = win.u[s, comp, layer + 1, tile]
                    elif layer == win.layers - 1:
                        radial = win.u[s, comp, layer - 1, tile]
                    else:
                        radial = win.u[s, comp, layer - 1, tile] + win.u[s, comp, layer + 1, tile]
                    elastic = (COEF_AXIAL * around + COEF_RADIAL * radial) - (
                        2.0 * (COEF_AXIAL + COEF_CIRC + COEF_RADIAL)
                    ) * u[comp]
                    visc = win.q[s, comp, layer, tile]
                    force = elastic + visc
                    if fiber[comp] is not None:
                        force = force + fiber[comp]
                    elif layer == 0:
                        force = force + win.load[s]
                    vel = win.v[s, comp, layer, tile]
                    vel = vel + (win.static[MASS, layer, tile] * force - win.static[DAMP, layer, tile] * vel)
                    win.v[s + 1, comp, layer, tile] = vel
                    win.u[s + 1, comp, layer, tile] = u[comp] + vel
                    win.q[s + 1, comp, layer, tile] = (
                        win.static[DECAY, layer, tile] * visc + win.static[SHARE, layer, tile] * elastic
                    )
        return carry

    lax.fori_loop(0, STEPS, step, 0)


def put_maps(win, tiles, end, keep_ref, send_ref):
    core = lax.rem(lax.axis_index("tm"), CORES)
    half = win.layers // CORES
    for layer in range(win.layers):
        for tile in tiles:
            weight = end(lambda w: w.weight.at[0], layer, tile)
            g = coarse(win.static[MASS, layer, tile], win.static[DAMP, layer, tile], win.static[STIFF, layer, tile], weight)
            pieces = [weight]
            start = [(win.u[0, comp, layer, tile], win.v[0, comp, layer, tile]) for comp in range(3)]
            for comp, (disp, vel) in enumerate(start):
                pieces.append(end(lambda w: w.u.at[STEPS, comp], layer, tile) - (g[0] * disp + g[1] * vel))
            for comp, (disp, vel) in enumerate(start):
                pieces.append(end(lambda w: w.v.at[STEPS, comp], layer, tile) - (g[2] * disp + g[3] * vel))
            to = (layer % half) * win.tiles + tile
            sent = (layer % half) * len(tiles) + tile - tiles[0]

            @pl.when(core == layer // half)
            def _():
                for k, piece in enumerate(pieces):
                    keep_ref[k, to] = piece

            @pl.when(core != layer // half)
            def _():
                for k, piece in enumerate(pieces):
                    send_ref[k, sent] = piece


def inner_kernel(*refs):
    fields, family_ref, pressure_ref, outs = refs[:7], refs[7], refs[8], refs[9:12]
    win = Window(refs[12:20])
    facing_ref = refs[20]
    states, statics, family_s, pressure_s, sem = refs[21:]
    tiles, cols, layers = win.tiles, win.cols, win.layers
    blocks = family_ref.shape[0]
    copies = []
    for k in range(3):
        copies.append(pltpu.make_async_copy(fields[k].at[0], states.at[k], sem.at[k]))
    for k in range(4):
        copies.append(pltpu.make_async_copy(fields[3 + k], statics.at[k], sem.at[3 + k]))
    directions = pltpu.make_async_copy(family_ref, family_s, sem.at[7])
    loads = pltpu.make_async_copy(pressure_ref, pressure_s, sem.at[8])
    for copy in (directions, loads, *copies):
        copy.start()
    directions.wait()
    loads.wait()
    for tile in range(tiles):
        win.dirs[0, tile], win.dirs[1, tile] = direction_tile(
            family_s, (2 * tile + blocks - 1) % blocks, 2 * tile, cols
        )
    facing_ref[0], facing_ref[1] = win.dirs[0, 0], win.dirs[1, 0]
    for s in range(STEPS):
        win.load[s] = jnp.full((8, cols), pressure_s[0, s], F32)

    def rolled(source, target):
        rows = [pltpu.roll(source[8 * tile : 8 * tile + 8, :], 4, 0) for tile in range(tiles)]
        for tile in range(tiles):
            target[tile] = jnp.where(low_rows(cols), rows[tile - 1], rows[tile])

    for k, target in enumerate((win.u, win.v, win.q)):
        copies[k].wait()
        for comp in range(3):
            for layer in range(layers):
                rolled(states.at[k, comp, layer], target.at[0, comp, layer])
    for k in range(4):
        copies[3 + k].wait()
        for layer in range(layers):
            rolled(statics.at[k, layer], win.static.at[k, layer])
    prepare(win, lambda tile, pairs: pairs[tile - 1])
    fine_steps(
        win, [*range(1, tiles), 0],
        lambda s, comp, layer, tile: win.u[s, comp, layer, (tile + tiles - 1) % tiles],
        lambda s, comp, layer, tile: win.u[s, comp, layer, (tile + 1) % tiles],
        None,
    )
    keep_ref, send_ref, visc_ref = outs
    put_maps(win, range(1, tiles), lambda of, layer, tile: of(win)[layer, tile], keep_ref, send_ref)
    for comp in range(3):
        for layer in range(layers):
            found = [win.q[STEPS, comp, layer, tile] for tile in range(1, tiles)]
            for k in range(tiles - 2):
                rows = slice(8 * k + 8, 8 * k + 16)
                visc_ref[comp, layer, rows, :] = own_rows(found[k], found[k + 1])


def outer_kernel(*refs):
    next_ref, prev_ref = refs[:2]
    inner = Window(refs[2:10])
    facing_ref = refs[12]
    outs = refs[13:16]
    win = Window(refs[16:])
    layers, cols = win.layers, win.cols
    place = lax.axis_index("space")
    has_next = place < lax.axis_size("space") - 1
    has_prev = place > 0
    low = low_rows(cols)
    live = jnp.where(low, has_prev.astype(jnp.int32), has_next.astype(jnp.int32)) > 0

    def halo(at, own, target):
        after, before = next_ref[at], prev_ref[at]
        for j in range(2):
            ahead = pltpu.roll(after, 4, 0) if j == 0 else after
            behind = before if j == 0 else pltpu.roll(before, 4, 0)
            target(j)[0] = jnp.where(low, own(j), jnp.where(live, ahead, 0.0))
            target(j)[1] = jnp.where(low, jnp.where(live, behind, 0.0), own(j))

    at = 0
    for source, target in ((inner.u, win.u), (inner.v, win.v), (inner.q, win.q)):
        for comp in range(3):
            for layer in range(0, layers, 2):
                halo(at, lambda j: source[0, comp, layer + j, 0], lambda j: target.at[0, comp, layer + j])
                at += 1
    for k in (MASS, DAMP, RATE, STIFF):
        for layer in range(0, layers, 2):
            halo(at, lambda j: inner.static[k, layer + j, 0], lambda j: win.static.at[k, layer + j])
            at += 1
    halo(at, lambda j: facing_ref[j], lambda j: win.dirs.at[j])
    for s in range(STEPS):
        win.load[s] = inner.load[s]
    last = inner.tiles - 1
    prepare(win, lambda tile, pairs: (inner.dirs[0, last], inner.dirs[1, last]))
    fine_steps(
        win, [0, 1],
        lambda s, comp, layer, tile: inner.u[s, comp, layer, last],
        lambda s, comp, layer, tile: inner.u[s, comp, layer, 1],
        lambda s, layer, tile, own: inner.sigma[s, layer, last],
    )

    def end(of, layer, tile):
        return jnp.where(low, of(win)[layer, 0], of(win)[layer, 1])

    keep_ref, send_ref, visc_ref = outs
    put_maps(inner, [0], end, keep_ref, send_ref)
    rows = visc_ref.shape[2]
    for comp in range(3):
        for layer in range(layers):
            facing = end(lambda w: w.q.at[STEPS, comp], layer, 0)
            visc_ref[comp, layer, 0:8, :] = own_rows(facing, inner.q[STEPS, comp, layer, 1])
            visc_ref[comp, layer, rows - 8 : rows, :] = own_rows(inner.q[STEPS, comp, layer, last], facing)


class Cut:
    def __init__(self, group, half, tiles, cols):
        self.group, self.half, self.tiles, self.cols = group, half, tiles, cols
        self.count = half * tiles
        self.size = self.count // group

    def of(self, part):
        first = part * self.size
        core = lax.rem(lax.axis_index("tm"), CORES)
        return first, core * self.half + first // self.tiles, lax.rem(first, self.tiles)

    def place(self):
        return lax.rem(lax.axis_index("tm") // CORES, self.group)


def sent_tile(facing_ref, rest_ref, cut, k, unit, tile):
    layer = unit // cut.tiles
    rest = rest_ref[k, layer * (cut.tiles - 1) + jnp.maximum(tile, 1) - 1]
    return jnp.where(tile == 0, facing_ref[k, layer], rest)


def part_coarse(static_ref, layer, tile, weight):
    return coarse(static_ref[MASS, layer, tile], static_ref[DAMP, layer, tile], static_ref[STIFF, layer, tile], weight)


def compose_kernel(cut, keep_ref, facing_ref, rest_ref, static_ref, *outs):
    first_core = lax.rem(lax.axis_index("tm"), CORES) == 0
    for m in range(cut.group):
        first, layer, tile = cut.of(jnp.bitwise_xor(cut.place(), m))
        for i in range(cut.size):
            keep = [keep_ref[k, first + i] for k in range(7)]
            got = [sent_tile(facing_ref, rest_ref, cut, k, first + i, tile + i) for k in range(7)]
            early = [jnp.where(first_core, a, b) for a, b in zip(keep, got)]
            late = [jnp.where(first_core, b, a) for a, b in zip(keep, got)]
            g = part_coarse(static_ref, layer, tile + i, late[0])
            outs[m][0, i] = early[0]
            outs[m][1, i] = late[0]
            for comp in range(3):
                a, b = early[1 + comp], early[4 + comp]
                outs[m][2 + comp, i] = (g[0] * a + g[1] * b) + late[1 + comp]
                outs[m][5 + comp, i] = (g[2] * a + g[3] * b) + late[4 + comp]


def chain(cut, parts, maps, static_ref, start, visit):
    place = cut.place()
    _, layer, tile = cut.of(place)
    for m in range(cut.group):
        maps[jnp.bitwise_xor(place, m)] = parts[m][...]
    for i in range(cut.size):
        state = [start(k, layer, tile + i, i) for k in range(6)]
        for s in range(cut.group):
            visit(s, i, state)
            first = part_coarse(static_ref, layer, tile + i, maps[s, 0, i])
            second = part_coarse(static_ref, layer, tile + i, maps[s, 1, i])
            new = [None] * 6
            for comp in range(3):
                a, b = state[comp], state[3 + comp]
                a, b = first[0] * a + first[1] * b, first[2] * a + first[3] * b
                new[comp] = (second[0] * a + second[1] * b) + maps[s, 2 + comp, i]
                new[3 + comp] = (second[2] * a + second[3] * b) + maps[s, 5 + comp, i]
            state = new
        visit(cut.group, i, state)


def first_state(cut, init_ref):
    def start(k, layer, tile, i):
        def load(t):
            return init_ref[k // 3, k % 3, layer, pl.ds(pl.multiple_of(8 * t, 8), 8), :]

        return rolled_tile(load, tile, cut.tiles, cut.cols)

    return start


def lower_kernel(cut, *refs):
    parts = refs[: cut.group]
    static_ref, init_ref, out_ref, maps = refs[cut.group :]

    def visit(s, i, state):
        if s == cut.group:
            for k in range(6):
                out_ref[k, i] = state[k]

    chain(cut, parts, maps, static_ref, first_state(cut, init_ref), visit)


def upper_kernel(cut, *refs):
    parts = refs[: cut.group]
    static_ref, init_ref, hop_ref = refs[cut.group : cut.group + 3]
    outs = refs[cut.group + 3 : 2 * cut.group + 3]
    maps, found = refs[2 * cut.group + 3 :]
    lower = lax.axis_index("tm") < CORES * cut.group
    first = first_state(cut, init_ref)

    def start(k, layer, tile, i):
        return jnp.where(lower, first(k, layer, tile, i), hop_ref[k, i])

    def visit(s, i, state):
        if s < cut.group:
            for k in range(6):
                found[s, k, i] = state[k]

    chain(cut, parts, maps, static_ref, start, visit)
    for m in range(cut.group):
        outs[m][...] = found[jnp.bitwise_xor(cut.place(), m)]


def spread_kernel(cut, *refs):
    parts = refs[: cut.group]
    keep_ref, facing_ref, rest_ref, static_ref, mine_ref, send_ref = refs[cut.group :]
    first_core = lax.rem(lax.axis_index("tm"), CORES) == 0
    for m in range(cut.group):
        first, layer, tile = cut.of(jnp.bitwise_xor(cut.place(), m))
        for i in range(cut.size):
            got = [sent_tile(facing_ref, rest_ref, cut, k, first + i, tile + i) for k in range(7)]
            early = [jnp.where(first_core, keep_ref[k, first + i], got[k]) for k in range(7)]
            g = part_coarse(static_ref, layer, tile + i, early[0])
            for comp in range(3):
                a, b = parts[m][comp, i], parts[m][3 + comp, i]
                next_a = (g[0] * a + g[1] * b) + early[1 + comp]
                next_b = (g[2] * a + g[3] * b) + early[4 + comp]
                mine_ref[comp, first + i] = jnp.where(first_core, a, next_a)
                mine_ref[3 + comp, first + i] = jnp.where(first_core, b, next_b)
                send_ref[comp, first + i] = jnp.where(first_core, next_a, a)
                send_ref[3 + comp, first + i] = jnp.where(first_core, next_b, b)


def unroll(load, store, tiles, cols):
    rows = [pltpu.roll(load(tile), 4, 0) for tile in range(tiles)]
    for tile in range(tiles):
        store(slice(8 * tile, 8 * tile + 8), jnp.where(low_rows(cols), rows[tile], rows[(tile + 1) % tiles]))


def join_kernel(cut, other, *refs):
    part_ref, (disp_ref, vel_ref, block, sem) = refs[0], refs[-4:]
    core = lax.rem(lax.axis_index("tm"), CORES)
    place = 1 - core if other else core
    copies = []
    for k in range(6):
        for layer in range(cut.half):
            def store(rows, value):
                block[k, layer, rows, :] = value

            unroll(lambda tile: part_ref[k, layer * cut.tiles + tile], store, cut.tiles, cut.cols)
        target = (disp_ref, vel_ref)[k // 3].at[0, k % 3, pl.ds(place * cut.half, cut.half)]
        copies.append(pltpu.make_async_copy(block.at[k], target, sem.at[k]))
        copies[-1].start()
    for copy in copies:
        copy.wait()


def swap_cores(value):
    count = lax.axis_size("tm")
    return lax.ppermute(value, "tm", [(i, i ^ 1) for i in range(count)])


def transpose_parts(parts):
    count = lax.axis_size("tm")
    done = [parts[0]]
    for m in range(1, len(parts)):
        done.append(lax.ppermute(parts[m], "tm", [(i, i ^ (CORES * m)) for i in range(count)]))
    return done


def shards(
    start_disp, start_vel, start_visc, init_state, inv_mass, damping_rate, visc_rate, fiber_stiff,
    fiber_family, pressure,
):
    slabs, spaces = lax.axis_size("tm"), lax.axis_size("space")
    group = slabs // CORES // 2
    layers, rows, cols = inv_mass.shape
    half, tiles = layers // CORES, rows // 8
    cut = Cut(group, half, tiles, cols)

    packed = shape((9 * layers + 4 * layers + 2) // 2, 8, cols)
    sides = ("facing",) if spaces == 2 else ("tail", "head")
    in_hbm = [
        pltpu.with_memory_space_constraint(x, pltpu.HBM)
        for x in (
            start_disp, start_vel, start_visc, inv_mass, damping_rate, visc_rate, fiber_stiff, fiber_family, pressure
        )
    ]
    packs = call(
        functools.partial(pack_kernel, sides),
        [packed] * len(sides),
        in_hbm[:8],
        [
            pltpu.VMEM((3, 3, layers, 8, cols), F32),
            pltpu.VMEM((4, layers, 8, cols), F32),
            pltpu.SMEM(fiber_family.shape, jnp.int32),
            pltpu.SemaphoreType.DMA((8,)),
        ],
        in_hbm=range(8),
    )
    if spaces == 2:
        after = before = lax.ppermute(packs[0], "space", [(0, 1), (1, 0)])
    else:
        before = lax.ppermute(packs[0], "space", [(i, i + 1) for i in range(spaces - 1)])
        after = lax.ppermute(packs[1], "space", [(i + 1, i) for i in range(spaces - 1)])

    map_shape = shape(7, cut.count, 8, cols)
    visc_shape = shape(3, layers, rows, cols)
    outs = [map_shape, shape(7, half * (tiles - 1), 8, cols), visc_shape]
    held = [shape(*dims) for dims in Window.shapes(layers, tiles, cols)]
    partial = call(
        inner_kernel,
        outs + held + [shape(2, 8, cols)],
        in_hbm,
        [
            pltpu.VMEM((3, 3, layers, rows, cols), F32),
            pltpu.VMEM((4, layers, rows, cols), F32),
            pltpu.SMEM(fiber_family.shape, jnp.int32),
            pltpu.SMEM(pressure.shape, F32),
            pltpu.SemaphoreType.DMA((9,)),
        ],
        in_hbm=range(9),
    )
    (keep, rest, end_visc), held, facing = partial[:3], partial[3:11], partial[11]
    before, rest = lax.optimization_barrier((before, rest))
    after = before if spaces == 2 else after
    rest = swap_cores(rest)
    keep, send, end_visc = call(
        outer_kernel,
        [map_shape, shape(7, half, 8, cols), visc_shape],
        (after, before, *held, keep, end_visc, facing),
        [pltpu.VMEM(dims, F32) for dims in Window.shapes(layers, 2, cols)],
        aliases={10: 0, 11: 2},
    )
    static = held[5]
    got = (swap_cores(send), rest)
    visc = lax.ppermute(end_visc, "tm", [(i, i + 1) for i in range(slabs - 1)])

    parts = call(
        functools.partial(compose_kernel, cut), [shape(8, cut.size, 8, cols)] * group, (keep, *got, static)
    )
    parts = transpose_parts(parts)
    maps = pltpu.VMEM((group, 8, cut.size, 8, cols), F32)
    edge = call(
        functools.partial(lower_kernel, cut), shape(6, cut.size, 8, cols), (*parts, static, init_state), [maps]
    )
    hop = lax.ppermute(edge, "tm", [(i, i ^ (slabs // 2)) for i in range(slabs)])
    states = call(
        functools.partial(upper_kernel, cut),
        [shape(6, cut.size, 8, cols)] * group,
        (*parts, static, init_state, hop),
        [maps, pltpu.VMEM((group, 6, cut.size, 8, cols), F32)],
    )
    states = transpose_parts(states)
    mine, other = call(
        functools.partial(spread_kernel, cut), [shape(6, cut.count, 8, cols)] * 2, (*states, keep, *got, static)
    )
    other = swap_cores(other)
    field = pltpu.HBM((1, 3, layers, rows, cols), F32)
    scratch = [pltpu.VMEM((6, half, rows, cols), F32), pltpu.SemaphoreType.DMA((6,))]
    joined = call(functools.partial(join_kernel, cut, False), [field, field], (mine,), scratch, out_hbm=True)
    new_disp, new_vel = call(
        functools.partial(join_kernel, cut, True), [field, field], (other, *joined), scratch,
        in_hbm=(1, 2), out_hbm=True, aliases={1: 0, 2: 1},
    )
    new_visc = jnp.where(lax.axis_index("tm") == 0, init_state[2], visc)[None]
    return new_disp, new_vel, new_visc


def solution(mesh):
    slab = P("tm", None, None, "space", None)
    cell = P(None, "space", None)
    return jax.shard_map(
        shards,
        mesh=mesh,
        in_specs=(
            slab, slab, slab, P(None, None, None, "space", None), cell, cell, cell, cell,
            P("space", None), P("tm", None),
        ),
        out_specs=(slab, slab, slab),
        check_vma=False,
    )
```

```python
import functools
import math

import jax
import jax.numpy as jnp
from jax import lax
from jax.experimental import pallas as pl
from jax.experimental.pallas import tpu as pltpu
from jax.sharding import PartitionSpec as P

STEPS = 4
BLK_AX = 4
BLK_CIR = 32
COEF_AXIAL = 0.22
COEF_CIRC = 0.22
COEF_RADIAL = 0.12
VISC_SHARE = 0.6
TIME_STEP = 1.0
FIBER_ANGLES = (0.5, -0.5, 0.9, -0.9)
CORES = 2
HALO = STEPS
F32 = jnp.float32
VMEM_LIMIT = 24 * 1024 * 1024


def call(kernel, out_shape, operands, scratch=(), in_hbm=(), out_hbm=False, aliases={}):
    specs = []
    for k in range(len(operands)):
        specs.append(pl.BlockSpec(memory_space=pltpu.HBM if k in in_hbm else pltpu.VMEM))
    return pl.pallas_call(
        kernel,
        out_shape=out_shape,
        in_specs=specs,
        out_specs=jax.tree.map(lambda _: pl.BlockSpec(memory_space=pltpu.HBM if out_hbm else pltpu.VMEM), out_shape),
        scratch_shapes=list(scratch),
        compiler_params=pltpu.CompilerParams(vmem_limit_bytes=VMEM_LIMIT),
        input_output_aliases=aliases,
    )(*operands)


def shape(*dims):
    return jax.ShapeDtypeStruct(dims, F32)


def iota(dims, axis):
    return lax.broadcasted_iota(jnp.int32, dims, axis)


def low_rows(cols):
    return iota((8, cols), 0) < HALO


def rolled_tile(load, tile, tiles, cols):
    last = (tile + tiles - 1) % tiles if isinstance(tile, int) else lax.rem(tile + tiles - 1, tiles)
    return jnp.where(low_rows(cols), pltpu.roll(load(last), 4, 0), pltpu.roll(load(tile), 4, 0))


def own_rows(first, second):
    return jnp.where(low_rows(first.shape[1]), pltpu.roll(first, 4, 0), pltpu.roll(second, 4, 0))


def direction_tile(family_ref, first, second, cols):
    block = iota((8, cols), 1) // BLK_CIR
    family = jnp.zeros((8, cols), jnp.int32)
    for k in range(cols // BLK_CIR):
        index = jnp.where(low_rows(cols), family_ref[first, k], family_ref[second, k])
        family = jnp.where(block == k, index, family)
    cosine = jnp.zeros((8, cols), F32)
    sine = jnp.zeros((8, cols), F32)
    for index, angle in enumerate(FIBER_ANGLES):
        cosine = jnp.where(family == index, math.cos(angle), cosine)
        sine = jnp.where(family == index, math.sin(angle), sine)
    return cosine, sine


def pack_kernel(sides, *refs):
    fields, family_ref = refs[:7], refs[7]
    outs = refs[8 : 8 + len(sides)]
    states, statics, family_s, sem = refs[8 + len(sides) :]
    rows, cols = fields[0].shape[-2:]
    block_rows = family_ref.shape[0]
    place = lax.axis_index("space")
    directions = pltpu.make_async_copy(family_ref, family_s, sem.at[7])
    for n, (out_ref, side) in enumerate(zip(outs, sides)):
        tail = (place == 0) if side == "facing" else jnp.bool_(side == "tail")
        start = pl.multiple_of(jnp.where(tail, rows - 8, 0), 8)
        copies = [] if n else [directions]
        for k in range(3):
            source = fields[k].at[0, :, :, pl.ds(start, 8), :]
            copies.append(pltpu.make_async_copy(source, states.at[k], sem.at[k]))
        for k in range(4):
            source = fields[3 + k].at[:, pl.ds(start, 8), :]
            copies.append(pltpu.make_async_copy(source, statics.at[k], sem.at[3 + k]))
        for copy in copies:
            copy.start()
        for copy in copies:
            copy.wait()
        low = low_rows(cols)

        def pair(first, second):
            up = pltpu.roll(first, 4, 0)
            down = pltpu.roll(second, 4, 0)
            return jnp.where(tail, jnp.where(low, up, second), jnp.where(low, first, down))

        at = 0
        for k in range(3):
            for comp in range(3):
                for layer in range(0, 4, 2):
                    out_ref[at] = pair(states[k, comp, layer], states[k, comp, layer + 1])
                    at += 1
        for k in range(4):
            for layer in range(0, 4, 2):
                out_ref[at] = pair(statics[k, layer], statics[k, layer + 1])
                at += 1
        end_block = jnp.where(tail, block_rows - 1, 0)
        cosine, sine = direction_tile(family_s, end_block, end_block, cols)
        out_ref[at] = jnp.where(low, cosine, sine)


def coarse(inv_mass, damping, stiff, weight):
    half_step = 0.5 * STEPS * TIME_STEP
    k = inv_mass * (2.0 * (COEF_AXIAL + COEF_CIRC + COEF_RADIAL) + 2.0 * stiff * weight)
    damp = half_step * damping
    square = half_step * half_step * k
    scale = 1.0 / (1.0 + damp + square)
    return (
        (1.0 + damp - square) * scale,
        (2.0 * half_step) * scale,
        (-2.0 * half_step) * k * scale,
        (1.0 - damp - square) * scale,
    )


class Window:
    def __init__(self, refs):
        self.u, self.v, self.q, self.sigma, self.weight, self.static, self.dirs, self.load = refs
        self.steps, _, self.layers, self.tiles, _, self.cols = self.u.shape

    @staticmethod
    def shapes(layers, tiles, cols):
        return (
            [(STEPS + 1, 3, layers, tiles, 8, cols)] * 3
            + [(STEPS, layers, tiles, 8, cols)] * 2
            + [(MASS_TO_SHARE, layers, tiles, 8, cols)]
            + [(9, tiles, 8, cols), (STEPS, 8, cols)]
        )


MASS, DAMP, RATE, STIFF, DECAY, SHARE, MASS_TO_SHARE = range(7)


def pred(a, before):
    return jnp.where(iota(a.shape, 0) == 0, pltpu.roll(before, 1, 0), pltpu.roll(a, 1, 0))


def succ(a, after):
    return jnp.where(iota(a.shape, 0) == 7, pltpu.roll(after, 7, 0), pltpu.roll(a, 7, 0))


def right(a):
    return pltpu.roll(a, a.shape[1] - 1, 1)


def left(a):
    return pltpu.roll(a, 1, 1)


def prepare(win, before_dirs):
    pairs = []
    for tile in range(win.tiles):
        cosine, sine = win.dirs[0, tile], win.dirs[1, tile]
        pairs.append((cosine * cosine, cosine * sine, sine * sine))
    for tile in range(win.tiles):
        cc, cs, ss = pairs[tile]
        before = before_dirs(tile, pairs)
        values = (cc, cs, ss, cc + cs, cs + ss, pred(cc, before[0]), pred(cs, before[1]), left(cs), left(ss))
        for k, value in enumerate(values):
            win.dirs[k, tile] = value
        for layer in range(win.layers):
            decay = jnp.exp(-TIME_STEP * win.static[RATE, layer, tile])
            win.static[DECAY, layer, tile] = decay
            win.static[SHARE, layer, tile] = (1.0 - decay) * VISC_SHARE


def fine_steps(win, order, before, after, before_sigma):
    def step(s, carry):
        def neighbours(layer, tile):
            u = [win.u[s, comp, layer, tile] for comp in range(3)]
            ahead = [succ(u[comp], after(s, comp, layer, tile)) for comp in range(3)]
            return u, ahead, [right(a) for a in u]

        def stress(layer, tile, u, ahead, beside):
            strain = (
                win.dirs[0, tile] * (ahead[1] - u[1])
                + win.dirs[2, tile] * (beside[2] - u[2])
                + win.dirs[1, tile] * ((ahead[2] - u[2]) + (beside[1] - u[1]))
            )
            weight = jnp.exp(strain * strain)
            sigma = win.static[STIFF, layer, tile] * weight * strain
            win.sigma[s, layer, tile] = sigma
            win.weight[s, layer, tile] = weight
            return sigma

        for layer in range(win.layers):
            known = {}
            if before_sigma is None:
                known[order[-1]] = stress(layer, order[-1], *neighbours(layer, order[-1]))
            for n, tile in enumerate(order):
                u, ahead, beside = neighbours(layer, tile)
                if tile not in known:
                    known[tile] = stress(layer, tile, u, ahead, beside)
                sigma = known[tile]
                last = known[order[n - 1]] if before_sigma is None else before_sigma(s, layer, tile, sigma)
                sigma_pred, sigma_left = pred(sigma, last), left(sigma)
                behind = [pred(u[comp], before(s, comp, layer, tile)) for comp in range(3)]
                fiber = [None] + [
                    win.dirs[3 + k, tile] * sigma
                    - win.dirs[5 + k, tile] * sigma_pred
                    - win.dirs[7 + k, tile] * sigma_left
                    for k in range(2)
                ]
                for comp in range(3):
                    around = (ahead[comp] + behind[comp]) + (beside[comp] + left(u[comp]))
                    if layer == 0:
                        radial = win.u[s, comp, layer + 1, tile]
                    elif layer == win.layers - 1:
                        radial = win.u[s, comp, layer - 1, tile]
                    else:
                        radial = win.u[s, comp, layer - 1, tile] + win.u[s, comp, layer + 1, tile]
                    elastic = (COEF_AXIAL * around + COEF_RADIAL * radial) - (
                        2.0 * (COEF_AXIAL + COEF_CIRC + COEF_RADIAL)
                    ) * u[comp]
                    visc = win.q[s, comp, layer, tile]
                    force = elastic + visc
                    if fiber[comp] is not None:
                        force = force + fiber[comp]
                    elif layer == 0:
                        force = force + win.load[s]
                    vel = win.v[s, comp, layer, tile]
                    vel = vel + (win.static[MASS, layer, tile] * force - win.static[DAMP, layer, tile] * vel)
                    win.v[s + 1, comp, layer, tile] = vel
                    win.u[s + 1, comp, layer, tile] = u[comp] + vel
                    win.q[s + 1, comp, layer, tile] = (
                        win.static[DECAY, layer, tile] * visc + win.static[SHARE, layer, tile] * elastic
                    )
        return carry

    lax.fori_loop(0, STEPS, step, 0)


def put_maps(win, tiles, end, keep_ref, send_ref):
    core = lax.rem(lax.axis_index("tm"), CORES)
    half = win.layers // CORES
    for layer in range(win.layers):
        for tile in tiles:
            weight = end(lambda w: w.weight.at[0], layer, tile)
            g = coarse(win.static[MASS, layer, tile], win.static[DAMP, layer, tile], win.static[STIFF, layer, tile], weight)
            pieces = [weight]
            start = [(win.u[0, comp, layer, tile], win.v[0, comp, layer, tile]) for comp in range(3)]
            for comp, (disp, vel) in enumerate(start):
                pieces.append(end(lambda w: w.u.at[STEPS, comp], layer, tile) - (g[0] * disp + g[1] * vel))
            for comp, (disp, vel) in enumerate(start):
                pieces.append(end(lambda w: w.v.at[STEPS, comp], layer, tile) - (g[2] * disp + g[3] * vel))
            to = (layer % half) * win.tiles + tile
            sent = (layer % half) * len(tiles) + tile - tiles[0]

            @pl.when(core == layer // half)
            def _():
                for k, piece in enumerate(pieces):
                    keep_ref[k, to] = piece

            @pl.when(core != layer // half)
            def _():
                for k, piece in enumerate(pieces):
                    send_ref[k, sent] = piece


def inner_kernel(*refs):
    fields, family_ref, pressure_ref, outs = refs[:7], refs[7], refs[8], refs[9:12]
    win = Window(refs[12:20])
    facing_ref = refs[20]
    states, statics, family_s, pressure_s, sem = refs[21:]
    tiles, cols, layers = win.tiles, win.cols, win.layers
    blocks = family_ref.shape[0]
    copies = []
    for k in range(3):
        copies.append(pltpu.make_async_copy(fields[k].at[0], states.at[k], sem.at[k]))
    for k in range(4):
        copies.append(pltpu.make_async_copy(fields[3 + k], statics.at[k], sem.at[3 + k]))
    directions = pltpu.make_async_copy(family_ref, family_s, sem.at[7])
    loads = pltpu.make_async_copy(pressure_ref, pressure_s, sem.at[8])
    for copy in (directions, loads, *copies):
        copy.start()
    directions.wait()
    loads.wait()
    for tile in range(tiles):
        win.dirs[0, tile], win.dirs[1, tile] = direction_tile(
            family_s, (2 * tile + blocks - 1) % blocks, 2 * tile, cols
        )
    facing_ref[0], facing_ref[1] = win.dirs[0, 0], win.dirs[1, 0]
    for s in range(STEPS):
        win.load[s] = jnp.full((8, cols), pressure_s[0, s], F32)

    def rolled(source, target):
        rows = [pltpu.roll(source[8 * tile : 8 * tile + 8, :], 4, 0) for tile in range(tiles)]
        for tile in range(tiles):
            target[tile] = jnp.where(low_rows(cols), rows[tile - 1], rows[tile])

    for k, target in enumerate((win.u, win.v, win.q)):
        copies[k].wait()
        for comp in range(3):
            for layer in range(layers):
                rolled(states.at[k, comp, layer], target.at[0, comp, layer])
    for k in range(4):
        copies[3 + k].wait()
        for layer in range(layers):
            rolled(statics.at[k, layer], win.static.at[k, layer])
    prepare(win, lambda tile, pairs: pairs[tile - 1])
    fine_steps(
        win, [*range(1, tiles), 0],
        lambda s, comp, layer, tile: win.u[s, comp, layer, (tile + tiles - 1) % tiles],
        lambda s, comp, layer, tile: win.u[s, comp, layer, (tile + 1) % tiles],
        None,
    )
    keep_ref, send_ref, visc_ref = outs
    put_maps(win, range(1, tiles), lambda of, layer, tile: of(win)[layer, tile], keep_ref, send_ref)
    for comp in range(3):
        for layer in range(layers):
            found = [win.q[STEPS, comp, layer, tile] for tile in range(1, tiles)]
            for k in range(tiles - 2):
                rows = slice(8 * k + 8, 8 * k + 16)
                visc_ref[comp, layer, rows, :] = own_rows(found[k], found[k + 1])


def outer_kernel(*refs):
    next_ref, prev_ref = refs[:2]
    inner = Window(refs[2:10])
    facing_ref = refs[12]
    outs = refs[13:16]
    win = Window(refs[16:])
    layers, cols = win.layers, win.cols
    place = lax.axis_index("space")
    has_next = place < lax.axis_size("space") - 1
    has_prev = place > 0
    low = low_rows(cols)
    live = jnp.where(low, has_prev.astype(jnp.int32), has_next.astype(jnp.int32)) > 0

    def halo(at, own, target):
        after, before = next_ref[at], prev_ref[at]
        for j in range(2):
            ahead = pltpu.roll(after, 4, 0) if j == 0 else after
            behind = before if j == 0 else pltpu.roll(before, 4, 0)
            target(j)[0] = jnp.where(low, own(j), jnp.where(live, ahead, 0.0))
            target(j)[1] = jnp.where(low, jnp.where(live, behind, 0.0), own(j))

    at = 0
    for source, target in ((inner.u, win.u), (inner.v, win.v), (inner.q, win.q)):
        for comp in range(3):
            for layer in range(0, layers, 2):
                halo(at, lambda j: source[0, comp, layer + j, 0], lambda j: target.at[0, comp, layer + j])
                at += 1
    for k in (MASS, DAMP, RATE, STIFF):
        for layer in range(0, layers, 2):
            halo(at, lambda j: inner.static[k, layer + j, 0], lambda j: win.static.at[k, layer + j])
            at += 1
    halo(at, lambda j: facing_ref[j], lambda j: win.dirs.at[j])
    for s in range(STEPS):
        win.load[s] = inner.load[s]
    last = inner.tiles - 1
    prepare(win, lambda tile, pairs: (inner.dirs[0, last], inner.dirs[1, last]))
    fine_steps(
        win, [0, 1],
        lambda s, comp, layer, tile: inner.u[s, comp, layer, last],
        lambda s, comp, layer, tile: inner.u[s, comp, layer, 1],
        lambda s, layer, tile, own: inner.sigma[s, layer, last],
    )

    def end(of, layer, tile):
        return jnp.where(low, of(win)[layer, 0], of(win)[layer, 1])

    keep_ref, send_ref, visc_ref = outs
    put_maps(inner, [0], end, keep_ref, send_ref)
    rows = visc_ref.shape[2]
    for comp in range(3):
        for layer in range(layers):
            facing = end(lambda w: w.q.at[STEPS, comp], layer, 0)
            visc_ref[comp, layer, 0:8, :] = own_rows(facing, inner.q[STEPS, comp, layer, 1])
            visc_ref[comp, layer, rows - 8 : rows, :] = own_rows(inner.q[STEPS, comp, layer, last], facing)


class Cut:
    def __init__(self, group, half, tiles, cols):
        self.group, self.half, self.tiles, self.cols = group, half, tiles, cols
        self.count = half * tiles
        self.size = self.count // group

    def of(self, part):
        first = part * self.size
        core = lax.rem(lax.axis_index("tm"), CORES)
        return first, core * self.half + first // self.tiles, lax.rem(first, self.tiles)

    def place(self):
        return lax.rem(lax.axis_index("tm") // CORES, self.group)


def sent_tile(facing_ref, rest_ref, cut, k, unit, tile):
    layer = unit // cut.tiles
    rest = rest_ref[k, layer * (cut.tiles - 1) + jnp.maximum(tile, 1) - 1]
    return jnp.where(tile == 0, facing_ref[k, layer], rest)


def part_coarse(static_ref, layer, tile, weight):
    return coarse(static_ref[MASS, layer, tile], static_ref[DAMP, layer, tile], static_ref[STIFF, layer, tile], weight)


def compose_kernel(cut, keep_ref, facing_ref, rest_ref, static_ref, *outs):
    first_core = lax.rem(lax.axis_index("tm"), CORES) == 0
    for m in range(cut.group):
        first, layer, tile = cut.of(jnp.bitwise_xor(cut.place(), m))
        for i in range(cut.size):
            keep = [keep_ref[k, first + i] for k in range(7)]
            got = [sent_tile(facing_ref, rest_ref, cut, k, first + i, tile + i) for k in range(7)]
            early = [jnp.where(first_core, a, b) for a, b in zip(keep, got)]
            late = [jnp.where(first_core, b, a) for a, b in zip(keep, got)]
            g = part_coarse(static_ref, layer, tile + i, late[0])
            outs[m][0, i] = early[0]
            outs[m][1, i] = late[0]
            for comp in range(3):
                a, b = early[1 + comp], early[4 + comp]
                outs[m][2 + comp, i] = (g[0] * a + g[1] * b) + late[1 + comp]
                outs[m][5 + comp, i] = (g[2] * a + g[3] * b) + late[4 + comp]


def order_kernel(cut, *refs):
    parts = refs[: cut.group]
    static_ref, out_ref = refs[cut.group :]
    place = cut.place()
    _, layer, tile = cut.of(place)
    for m in range(cut.group):
        to = jnp.bitwise_xor(place, m)
        for i in range(cut.size):
            for j in range(2):
                g = part_coarse(static_ref, layer, tile + i, parts[m][j, i])
                for k in range(4):
                    out_ref[to, 4 * j + k, i] = g[k]
            for k in range(6):
                out_ref[to, 8 + k, i] = parts[m][2 + k, i]


def chain(cut, maps, start, visit):
    _, layer, tile = cut.of(cut.place())
    for i in range(cut.size):
        state = [start(k, layer, tile + i, i) for k in range(6)]
        for s in range(cut.group):
            visit(s, i, state)
            first = [maps[s, k, i] for k in range(4)]
            second = [maps[s, 4 + k, i] for k in range(4)]
            new = [None] * 6
            for comp in range(3):
                a, b = state[comp], state[3 + comp]
                a, b = first[0] * a + first[1] * b, first[2] * a + first[3] * b
                new[comp] = (second[0] * a + second[1] * b) + maps[s, 8 + comp, i]
                new[3 + comp] = (second[2] * a + second[3] * b) + maps[s, 11 + comp, i]
            state = new
        visit(cut.group, i, state)


def first_state(cut, init_ref):
    def start(k, layer, tile, i):
        def load(t):
            return init_ref[k // 3, k % 3, layer, pl.ds(pl.multiple_of(8 * t, 8), 8), :]

        return rolled_tile(load, tile, cut.tiles, cut.cols)

    return start


def lower_kernel(cut, *refs):
    parts, (static_ref, init_ref, out_ref, maps) = refs[: cut.group], refs[cut.group :]
    order_kernel(cut, *parts, static_ref, maps)

    def visit(s, i, state):
        if s == cut.group:
            for k in range(6):
                out_ref[k, i] = state[k]

    chain(cut, maps, first_state(cut, init_ref), visit)


def upper_kernel(cut, *refs):
    maps, init_ref, hop_ref = refs[:3]
    outs, found = refs[3 : cut.group + 3], refs[cut.group + 3]
    lower = lax.axis_index("tm") < CORES * cut.group
    first = first_state(cut, init_ref)

    def start(k, layer, tile, i):
        return jnp.where(lower, first(k, layer, tile, i), hop_ref[k, i])

    def visit(s, i, state):
        if s < cut.group:
            for k in range(6):
                found[s, k, i] = state[k]

    chain(cut, maps, start, visit)
    for m in range(cut.group):
        outs[m][...] = found[jnp.bitwise_xor(cut.place(), m)]


def spread_kernel(cut, *refs):
    parts = refs[: cut.group]
    keep_ref, facing_ref, rest_ref, static_ref, mine_ref, send_ref = refs[cut.group :]
    first_core = lax.rem(lax.axis_index("tm"), CORES) == 0
    for m in range(cut.group):
        first, layer, tile = cut.of(jnp.bitwise_xor(cut.place(), m))
        for i in range(cut.size):
            got = [sent_tile(facing_ref, rest_ref, cut, k, first + i, tile + i) for k in range(7)]
            early = [jnp.where(first_core, keep_ref[k, first + i], got[k]) for k in range(7)]
            g = part_coarse(static_ref, layer, tile + i, early[0])
            for comp in range(3):
                a, b = parts[m][comp, i], parts[m][3 + comp, i]
                next_a = (g[0] * a + g[1] * b) + early[1 + comp]
                next_b = (g[2] * a + g[3] * b) + early[4 + comp]
                mine_ref[comp, first + i] = jnp.where(first_core, a, next_a)
                mine_ref[3 + comp, first + i] = jnp.where(first_core, b, next_b)
                send_ref[comp, first + i] = jnp.where(first_core, next_a, a)
                send_ref[3 + comp, first + i] = jnp.where(first_core, next_b, b)


def unroll(load, store, tiles, cols):
    rows = [pltpu.roll(load(tile), 4, 0) for tile in range(tiles)]
    for tile in range(tiles):
        store(slice(8 * tile, 8 * tile + 8), jnp.where(low_rows(cols), rows[tile], rows[(tile + 1) % tiles]))


def join_kernel(cut, other, *refs):
    part_ref, (disp_ref, vel_ref, block, sem) = refs[0], refs[-4:]
    core = lax.rem(lax.axis_index("tm"), CORES)
    place = 1 - core if other else core
    copies = []
    for k in range(6):
        for layer in range(cut.half):
            def store(rows, value):
                block[k, layer, rows, :] = value

            unroll(lambda tile: part_ref[k, layer * cut.tiles + tile], store, cut.tiles, cut.cols)
        target = (disp_ref, vel_ref)[k // 3].at[0, k % 3, pl.ds(place * cut.half, cut.half)]
        copies.append(pltpu.make_async_copy(block.at[k], target, sem.at[k]))
        copies[-1].start()
    for copy in copies:
        copy.wait()


def swap_cores(value):
    count = lax.axis_size("tm")
    return lax.ppermute(value, "tm", [(i, i ^ 1) for i in range(count)])


def transpose_parts(parts):
    count = lax.axis_size("tm")
    done = [parts[0]]
    for m in range(1, len(parts)):
        done.append(lax.ppermute(parts[m], "tm", [(i, i ^ (CORES * m)) for i in range(count)]))
    return done


def shards(
    start_disp, start_vel, start_visc, init_state, inv_mass, damping_rate, visc_rate, fiber_stiff,
    fiber_family, pressure,
):
    slabs, spaces = lax.axis_size("tm"), lax.axis_size("space")
    group = slabs // CORES // 2
    layers, rows, cols = inv_mass.shape
    half, tiles = layers // CORES, rows // 8
    cut = Cut(group, half, tiles, cols)

    packed = shape((9 * layers + 4 * layers + 2) // 2, 8, cols)
    sides = ("facing",) if spaces == 2 else ("tail", "head")
    in_hbm = [
        pltpu.with_memory_space_constraint(x, pltpu.HBM)
        for x in (
            start_disp, start_vel, start_visc, inv_mass, damping_rate, visc_rate, fiber_stiff, fiber_family, pressure
        )
    ]
    packs = call(
        functools.partial(pack_kernel, sides),
        [packed] * len(sides),
        in_hbm[:8],
        [
            pltpu.VMEM((3, 3, layers, 8, cols), F32),
            pltpu.VMEM((4, layers, 8, cols), F32),
            pltpu.SMEM(fiber_family.shape, jnp.int32),
            pltpu.SemaphoreType.DMA((8,)),
        ],
        in_hbm=range(8),
    )
    if spaces == 2:
        after = before = lax.ppermute(packs[0], "space", [(0, 1), (1, 0)])
    else:
        before = lax.ppermute(packs[0], "space", [(i, i + 1) for i in range(spaces - 1)])
        after = lax.ppermute(packs[1], "space", [(i + 1, i) for i in range(spaces - 1)])

    map_shape = shape(7, cut.count, 8, cols)
    visc_shape = shape(3, layers, rows, cols)
    outs = [map_shape, shape(7, half * (tiles - 1), 8, cols), visc_shape]
    held = [shape(*dims) for dims in Window.shapes(layers, tiles, cols)]
    partial = call(
        inner_kernel,
        outs + held + [shape(2, 8, cols)],
        in_hbm,
        [
            pltpu.VMEM((3, 3, layers, rows, cols), F32),
            pltpu.VMEM((4, layers, rows, cols), F32),
            pltpu.SMEM(fiber_family.shape, jnp.int32),
            pltpu.SMEM(pressure.shape, F32),
            pltpu.SemaphoreType.DMA((9,)),
        ],
        in_hbm=range(9),
    )
    (keep, rest, end_visc), held, facing = partial[:3], partial[3:11], partial[11]
    before, rest = lax.optimization_barrier((before, rest))
    after = before if spaces == 2 else after
    rest = swap_cores(rest)
    keep, send, end_visc = call(
        outer_kernel,
        [map_shape, shape(7, half, 8, cols), visc_shape],
        (after, before, *held, keep, end_visc, facing),
        [pltpu.VMEM(dims, F32) for dims in Window.shapes(layers, 2, cols)],
        aliases={10: 0, 11: 2},
    )
    static = held[5]
    got = (swap_cores(send), rest)
    visc = lax.ppermute(end_visc, "tm", [(i, i + 1) for i in range(slabs - 1)])

    parts = call(
        functools.partial(compose_kernel, cut), [shape(8, cut.size, 8, cols)] * group, (keep, *got, static)
    )
    parts = transpose_parts(parts)
    edge, maps = call(
        functools.partial(lower_kernel, cut),
        [shape(6, cut.size, 8, cols), shape(group, 14, cut.size, 8, cols)],
        (*parts, static, init_state),
    )
    hop = lax.ppermute(edge, "tm", [(i, i ^ (slabs // 2)) for i in range(slabs)])
    states = call(
        functools.partial(upper_kernel, cut),
        [shape(6, cut.size, 8, cols)] * group,
        (maps, init_state, hop),
        [pltpu.VMEM((group, 6, cut.size, 8, cols), F32)],
    )
    states = transpose_parts(states)
    mine, other = call(
        functools.partial(spread_kernel, cut), [shape(6, cut.count, 8, cols)] * 2, (*states, keep, *got, static)
    )
    other = swap_cores(other)
    field = pltpu.HBM((1, 3, layers, rows, cols), F32)
    scratch = [pltpu.VMEM((6, half, rows, cols), F32), pltpu.SemaphoreType.DMA((6,))]
    joined = call(functools.partial(join_kernel, cut, False), [field, field], (mine,), scratch, out_hbm=True)
    new_disp, new_vel = call(
        functools.partial(join_kernel, cut, True), [field, field], (other, *joined), scratch,
        in_hbm=(1, 2), out_hbm=True, aliases={1: 0, 2: 1},
    )
    new_visc = jnp.where(lax.axis_index("tm") == 0, init_state[2], visc)[None]
    return new_disp, new_vel, new_visc


def solution(mesh):
    slab = P("tm", None, None, "space", None)
    cell = P(None, "space", None)
    return jax.shard_map(
        shards,
        mesh=mesh,
        in_specs=(
            slab, slab, slab, P(None, None, None, "space", None), cell, cell, cell, cell,
            P("space", None), P("tm", None),
        ),
        out_specs=(slab, slab, slab),
        check_vma=False,
    )
```
